256 devices in a mesh: region: 64 (over y, x_hi, z), station: 4 (over x_lo, core).
Axes of the slice: x: 4 (x_hi: 2, x_lo: 2; x = x_hi * 2 + x_lo), y: 4, z: 8, core: 2. Of those that a mesh axis runs over, the one named last changes fastest.
Arguments:
- waveforms: bfloat16 [1024, 16, 3, 512], P('region', 'station'), may hold values from -6 to 6
- pair_lists: int32 [3, 2048, 2], P(None, 'region'), may hold values from 0 to 15
- pair_counts: int32 [3, 64], P(None, 'region'), may hold values from 1 to 32, as said below
Outputs:
- correlations: float32 [3, 2048, 256], P(None, ('region', 'station'))
The draws below stay inside these ranges and needn't reach their ends.
Inputs may be any that keep to these rules, and one draw needn't show every extreme that they name: `pair_counts`: in every round some region has all 32 slots live.
All inputs are finite; a program needn't handle non-finite values.
Results may differ from the reference program's by a relative error of at most 0.011.
Values may be sent and summed in bfloat16 or wider, within the bound.
A program may use at most 64 MiB of HBM per device.

```python
import math
import jax
import jax.numpy as jnp
from jax import lax

STATIONS = 16
COMP = 3
SAMPLES = 512
ROUNDS = 3
EV_DEV = 16
PAIR_DEV = 32
LAGS = 256
REGIONS = 64
EVENTS = 1024
PAIRS = 2048
N_REGION = 64
N_STATION = 4


def draw_pair_counts(key, part):
    first_key, second_key = jax.random.split(jax.random.fold_in(key, 7))
    counts = jax.random.randint(first_key, (ROUNDS, REGIONS), 1, PAIR_DEV + 1)
    fullest = jax.random.randint(second_key, (ROUNDS, 1), 0, REGIONS)
    region_ids = jnp.arange(REGIONS, dtype=jnp.int32)[None, :]
    return jnp.where(region_ids == fullest, PAIR_DEV, counts).astype(jnp.int32)


def place_ends(drawn, key, smallest, top_value):
    shape = drawn.shape
    place = [jax.random.randint(jax.random.fold_in(key, axis), (), 0, shape[axis]) for axis in range(len(shape))]
    drawn = drawn.at[tuple(place)].set(smallest)
    longest = shape.index(max(shape))
    place[longest] = (place[longest] + 1) % shape[longest]
    return drawn.at[tuple(place)].set(top_value)


def block_levels(rng, shape, cuts, least, high):
    gain = 1.0
    for axis_at, shards_of in cuts:
        heights = jax.random.uniform(jax.random.fold_in(jax.random.fold_in(rng, 6), axis_at), (shards_of,), jnp.float32, least / len(cuts), high / len(cuts))
        gain = gain * jnp.repeat(jnp.exp(heights), shape[axis_at] // shards_of).reshape((-1,) + (1,) * (len(shape) - 1 - axis_at))
    return gain


def normal_values(key, dims, scale, limit, cuts=(), kind=jnp.bfloat16):
    values = scale * jax.random.normal(key, dims, jnp.float32)
    if cuts:
        values = values * block_levels(key, dims, cuts, -0.22, 0.18)
    return jnp.clip(values, -limit, limit).astype(kind)


def setup_inputs(seed: int = 0) -> dict:
    key_of = jax.random.split(jax.random.key(seed), 4)
    return {
        "waveforms": normal_values(key_of[0], (EVENTS, STATIONS, COMP, SAMPLES), 1.0, 6.0, ((0, 64), (1, 4))),
        "pair_lists": place_ends(jax.random.randint(key_of[1], (ROUNDS, PAIRS, 2), 0, EV_DEV), jax.random.fold_in(key_of[1], 1), 0, EV_DEV - 1).astype(jnp.int32),
        "pair_counts": draw_pair_counts(jax.random.fold_in(key_of[3], 71), 0),
    }


TWO_PI = 2.0 * math.pi
EPS = 1e-06

def forward_table(length):
    period = 2 * length
    times = jnp.arange(length, dtype=jnp.int32)[:, None]
    freqs = jnp.arange(period, dtype=jnp.int32)[None, :]
    angle = TWO_PI / period * (times * freqs % period).astype(jnp.float32)
    return jnp.concatenate([jnp.cos(angle), -jnp.sin(angle)], axis=1).astype(jnp.bfloat16)

def inverse_table(length, channels):
    period = 2 * length
    half = length // 2
    freqs = jnp.arange(period, dtype=jnp.int32)[:, None]
    lagged = jnp.arange(half, dtype=jnp.int32)[None, :] - half // 2
    angle = TWO_PI / period * (freqs * lagged % period).astype(jnp.float32)
    factor = 1.0 / (period * math.sqrt(channels * length))
    return (jnp.concatenate([jnp.cos(angle), -jnp.sin(angle)], axis=0) * factor).astype(jnp.bfloat16)

def spectra_of(block):
    events, stations, comps, length = block.shape
    traces = block.astype(jnp.float32)
    traces = traces - lax.optimization_barrier(jnp.mean(traces, axis=-1, keepdims=True))
    traces = traces * lax.rsqrt(lax.optimization_barrier(jnp.mean(traces * traces, axis=-1, keepdims=True)) + EPS)
    traces = traces.astype(jnp.bfloat16).reshape(events * stations * comps, length)
    spec = jnp.dot(traces, forward_table(length), preferred_element_type=jnp.float32)
    return spec.astype(jnp.bfloat16).reshape(events, stations * comps, 4 * length)

def cross_curves(left, right, groups, lag_table):
    slots, channels, width = left.shape
    period = width // 2
    left_parts = left.reshape(slots, groups, channels // groups, 2, period).astype(jnp.float32)
    right_parts = right.reshape(slots, groups, channels // groups, 2, period).astype(jnp.float32)
    rotated = jnp.stack([right_parts[:, :, :, 1], -right_parts[:, :, :, 0]], axis=3)
    real_part = jnp.einsum('pgchk,pgchk->pgk', left_parts, right_parts)
    imag_part = jnp.einsum('pgchk,pgchk->pgk', left_parts, rotated)
    cross = jnp.concatenate([real_part, imag_part], axis=-1).astype(jnp.bfloat16)
    return jnp.einsum('pgf,fl->pl', cross.astype(jnp.float32), lag_table.astype(jnp.float32))

def reference(waveforms, pair_lists, pair_counts):
    blocks = waveforms.reshape(N_REGION, EV_DEV, STATIONS, COMP, SAMPLES)
    spectra = lax.map(spectra_of, blocks)
    lag_table = inverse_table(SAMPLES, STATIONS * COMP)
    outputs = []
    for round_index in range(ROUNDS):

        def region_block(region_id, round_index=round_index):
            partner = jnp.bitwise_xor(region_id, jnp.int32(1 << round_index))
            pair_rows = lax.dynamic_slice_in_dim(pair_lists[round_index], (region_id * PAIR_DEV).astype(jnp.int32), PAIR_DEV, 0)
            left = jnp.take(spectra[region_id], pair_rows[:, 0], axis=0)
            right = jnp.take(spectra[partner], pair_rows[:, 1], axis=0)
            curves = cross_curves(left, right, N_STATION, lag_table)
            live = jnp.arange(PAIR_DEV, dtype=jnp.int32) < pair_counts[round_index, region_id]
            return jnp.where(live[:, None], curves, jnp.zeros_like(curves))
        result = lax.map(region_block, jnp.arange(N_REGION, dtype=jnp.int32))
        outputs.append(result.reshape(PAIRS, LAGS))
    return jnp.stack(outputs)
```

```python
import functools
import math

import jax
import jax.numpy as jnp
import numpy as np
from jax import lax
from jax.experimental import pallas as pl
from jax.experimental.pallas import tpu as pltpu
from jax.sharding import PartitionSpec as P

MESH = pl.DeviceIdType.MESH
ROUNDS = 3
EVENTS = 16
GROUP = 4
COMP = 3
LENGTH = 512
LAGS = 256
SLOTS = 32
STATIONS = 16
EPS = 1e-06
CHUNK = COMP * EVENTS
TRACES = GROUP * CHUNK
PERIOD = LENGTH + LAGS // 2
HALF = PERIOD // 2
WIDE = 3 * LAGS
LOWER = (2, 2, 3)


def tables():
    order = np.arange(HALF)
    times = np.arange(LENGTH)[:, None]
    angle = 2.0 * np.pi * ((2 * order[None, :] + 1) * times % (2 * PERIOD)) / (2 * PERIOD)
    real, imag = np.cos(angle), -np.sin(angle)
    forward = np.concatenate([real[:, :256], imag[:, :256], real[:, 256:], imag[:, 256:]], axis=1)
    lags = np.arange(LAGS)[None, :] - LAGS // 2
    angle = 2.0 * np.pi * ((2 * order[:, None] + 1) * lags % (2 * PERIOD)) / (2 * PERIOD)
    factor = 2.0 / (PERIOD * math.sqrt(STATIONS * COMP * LENGTH))
    cos, sin = factor * np.cos(angle), factor * np.sin(angle)
    inverse = np.concatenate(
        [cos[:256], -sin[:256], cos[256:], cos[256:], -sin[256:], sin[256:]], axis=0
    )
    return forward.astype(jnp.bfloat16), inverse.astype(jnp.bfloat16)


def kernel(
    x_hbm, lists_ref, forward_hbm, inverse_hbm, out_ref,
    x_in, forward, inverse, normal, arrived, spectra, theirs, left, right, total,
    message, heard, picks, shares, gathered,
    load_sem, wave_out, wave_in, list_out, list_in, share_out, share_in, ready,
):
    region, group = lax.axis_index("region"), lax.axis_index("station")
    z = lax.rem(region, 8)
    upper = [lax.rem(z // (1 << e), 2) for e in range(ROUNDS)]
    partner = [region + (1 << e) * (1 - 2 * upper[e]) for e in range(ROUNDS)]
    mates = [lax.rem(group + d, GROUP) for d in range(GROUP)]
    late = upper[2]

    barrier = pltpu.get_barrier_semaphore()

    def greet(which, to):
        pl.semaphore_signal(which, inc=1, device_id=to, device_id_type=MESH)

    for d in range(1, GROUP):
        greet(barrier, (region, mates[d]))
    for e in range(2):
        for d in range(GROUP):
            greet(barrier, (partner[e], mates[d]))

    @pl.when(late == 0)
    def _():
        for d in range(GROUP):
            greet(barrier, (partner[2], mates[d]))

    loads = [
        pltpu.make_async_copy(x_hbm, x_in, load_sem.at[0]),
        pltpu.make_async_copy(forward_hbm, forward, load_sem.at[1]),
        pltpu.make_async_copy(inverse_hbm, inverse, load_sem.at[2]),
    ]
    for load in loads:
        load.start()

    message[...] = jnp.zeros_like(message)
    for e in range(ROUNDS):
        message[2 * e : 2 * e + 2, 0:SLOTS] = lists_ref[e]
    mine = message[...]
    turned = pltpu.roll(mine, SLOTS, 1)
    even = lax.rem(lax.broadcasted_iota(jnp.int32, (8, 128), 0), 2) == 0
    turned = jnp.where(even, pltpu.roll(turned, 7, 0), pltpu.roll(turned, 1, 0))
    message[...] = turned

    loads[0].wait()
    traces = x_in[...].astype(jnp.float32).reshape(TRACES, LENGTH)
    traces = traces - jnp.mean(traces, axis=-1, keepdims=True)
    traces = traces * lax.rsqrt(jnp.mean(traces * traces, axis=-1, keepdims=True) + EPS)
    row = lax.broadcasted_iota(jnp.int32, (TRACES, TRACES), 0)
    column = lax.broadcasted_iota(jnp.int32, (TRACES, TRACES), 1)
    source = lax.rem(row, EVENTS) * (COMP * GROUP) + lax.rem(row // EVENTS, COMP) * GROUP + row // CHUNK
    reorder = jnp.where(column == source, 1.0, 0.0).astype(jnp.bfloat16)
    normal[...] = jnp.dot(
        reorder, traces.astype(jnp.bfloat16), preferred_element_type=jnp.float32
    ).astype(jnp.bfloat16)

    def rows(s):
        return pl.ds(pl.multiple_of(s * CHUNK, CHUNK), CHUNK)

    def wave(e, s):
        return pltpu.make_async_remote_copy(
            src_ref=normal.at[rows(s)],
            dst_ref=arrived.at[e, rows(s)],
            send_sem=wave_out.at[e, s],
            recv_sem=wave_in.at[e, s],
            device_id=(partner[e], group),
            device_id_type=MESH,
        )

    def listing(e):
        return pltpu.make_async_remote_copy(
            src_ref=message,
            dst_ref=heard.at[e],
            send_sem=list_out.at[e],
            recv_sem=list_in.at[e],
            device_id=(partner[e], group),
            device_id_type=MESH,
        )

    def share(e, side, d):
        to = region if side == 0 else partner[e]
        return pltpu.make_async_remote_copy(
            src_ref=shares.at[e, GROUP * side + mates[d]],
            dst_ref=gathered.at[e, GROUP * side + group],
            send_sem=share_out.at[e, GROUP * side + mates[d]],
            recv_sem=share_in.at[e, GROUP * side + group],
            device_id=(to, mates[d]),
            device_id_type=MESH,
        )

    def landed(e, side, d):
        to = region if side == 0 else partner[e]
        return pltpu.make_async_remote_copy(
            src_ref=shares.at[e, GROUP * side + mates[d]],
            dst_ref=gathered.at[e, GROUP * side + mates[d]],
            send_sem=share_out.at[e, GROUP * side + mates[d]],
            recv_sem=share_in.at[e, GROUP * side + mates[d]],
            device_id=(to, mates[d]),
            device_id_type=MESH,
        )

    first = [upper[e] * LOWER[e] for e in range(ROUNDS)]
    count = [LOWER[e] + upper[e] * (GROUP - 2 * LOWER[e]) for e in range(ROUNDS)]
    first_sent = [(1 - upper[e]) * LOWER[e] for e in range(ROUNDS)]

    def send(e):
        listing(e).start()

        @pl.loop(0, GROUP - count[e])
        def _(i):
            wave(e, first_sent[e] + i).start()

    @pl.when(late == 0)
    def _():
        pl.semaphore_wait(barrier, 11)

    @pl.when(late == 1)
    def _():
        pl.semaphore_wait(barrier, 15)
        for d in range(GROUP):
            greet(ready, (partner[2], mates[d]))
        send(2)

    send(0)
    send(1)

    loads[1].wait()
    spectra[...] = jnp.dot(
        normal[...], forward[...], preferred_element_type=jnp.float32
    ).astype(jnp.bfloat16)
    loads[2].wait()

    lane = lax.broadcasted_iota(jnp.int32, (8, 128), 1)
    cell = lax.broadcasted_iota(jnp.int32, (COMP * 2 * SLOTS, CHUNK), 1)
    part = lax.broadcasted_iota(jnp.int32, (COMP * 2 * SLOTS, CHUNK), 0) // (2 * SLOTS) * EVENTS
    theirs_row = lax.broadcasted_iota(jnp.int32, (2 * SLOTS, LAGS), 0) >= SLOTS

    for e in range(ROUNDS):
        if e == 1:

            @pl.when(late == 0)
            def _():
                pl.semaphore_wait(ready, GROUP)
                send(2)

        listing(e).wait_recv()
        events = jnp.where(lane < SLOTS, mine, heard[e]).astype(jnp.float32).T
        for side in range(2):
            event = events[: 2 * SLOTS, 2 * e + side : 2 * e + side + 1].astype(jnp.int32)
            event = jnp.concatenate([event] * COMP, axis=0)
            picks[side] = jnp.where(cell == part + event, 1.0, 0.0).astype(jnp.bfloat16)
        total[...] = jnp.zeros_like(total)

        @pl.loop(0, count[e])
        def _(i, e=e):
            s = first[e] + i
            wave(e, s).wait_recv()
            theirs[...] = jnp.dot(
                arrived[e, rows(s)], forward[...], preferred_element_type=jnp.float32
            ).astype(jnp.bfloat16)
            left[...] = jnp.dot(picks[0], spectra[rows(s)], preferred_element_type=jnp.float32)
            right[...] = jnp.dot(picks[1], theirs[...], preferred_element_type=jnp.float32)
            for c in range(COMP):
                at = pl.ds(c * 2 * SLOTS, 2 * SLOTS)
                lr, li, lm = left[at, 0:256], left[at, 256:512], left[at, 512:640]
                rr, ri, rm = right[at, 0:256], right[at, 256:512], right[at, 512:640]
                total[:, 0:256] += lr * rr + li * ri
                total[:, 256:512] += lr * ri - li * rr
                total[:, 512:640] += lm * rm
                total[:, 640:768] += lm * pltpu.roll(rm, 64, 1)

        real, imag, both, cross = total[:, 0:256], total[:, 256:512], total[:, 512:640], total[:, 640:768]
        imag = jnp.where(theirs_row, -imag, imag)
        cross = jnp.where(theirs_row[:, :128], -cross, cross)
        curves = jnp.dot(
            jnp.concatenate([real, imag, both, cross], axis=1).astype(jnp.bfloat16),
            inverse[...],
            preferred_element_type=jnp.float32,
        )
        for k in range(2 * GROUP):
            piece = curves[8 * k : 8 * k + 8]
            shares[e, k] = jnp.concatenate([piece[:, :128], piece[:, 128:]], axis=0).astype(jnp.bfloat16)
        for d in range(GROUP):
            share(e, 1, d).start()
        for d in range(1, GROUP):
            share(e, 0, d).start()
        gathered[e, pl.ds(group, 1)] = shares[e, pl.ds(group, 1)]

    for e in range(ROUNDS):
        for d in range(1, GROUP):
            landed(e, 0, d).wait_recv()
        for d in range(GROUP):
            landed(e, 1, d).wait_recv()
        curve = jnp.sum(gathered[e].astype(jnp.float32), axis=0)
        out_ref[e, :, 0:128] = curve[0:8]
        out_ref[e, :, 128:256] = curve[8:16]

    for e in range(ROUNDS):
        listing(e).wait_send()

        @pl.loop(0, GROUP - count[e])
        def _(i, e=e):
            wave(e, first_sent[e] + i).wait_send()

        for d in range(1, GROUP):
            share(e, 0, d).wait_send()
        for d in range(GROUP):
            share(e, 1, d).wait_send()


def shards(waveforms, pair_lists, pair_counts):
    forward, inverse = tables()
    bf16, f32 = jnp.bfloat16, jnp.float32
    dma = pltpu.SemaphoreType.DMA
    curves = pl.pallas_call(
        kernel,
        out_shape=jax.ShapeDtypeStruct((ROUNDS, 8, LAGS), f32),
        in_specs=[
            pl.BlockSpec(memory_space=pl.ANY),
            pl.BlockSpec(memory_space=pltpu.VMEM),
            pl.BlockSpec(memory_space=pl.ANY),
            pl.BlockSpec(memory_space=pl.ANY),
        ],
        out_specs=pl.BlockSpec(memory_space=pltpu.VMEM),
        scratch_shapes=[
            pltpu.VMEM((EVENTS, COMP, GROUP, LENGTH), bf16),
            pltpu.VMEM((LENGTH, PERIOD), bf16),
            pltpu.VMEM((WIDE, LAGS), bf16),
            pltpu.VMEM((TRACES, LENGTH), bf16),
            pltpu.VMEM((ROUNDS, TRACES, LENGTH), bf16),
            pltpu.VMEM((TRACES, PERIOD), bf16),
            pltpu.VMEM((CHUNK, PERIOD), bf16),
            pltpu.VMEM((COMP * 2 * SLOTS, PERIOD), f32),
            pltpu.VMEM((COMP * 2 * SLOTS, PERIOD), f32),
            pltpu.VMEM((2 * SLOTS, WIDE), f32),
            pltpu.VMEM((8, 128), jnp.int32),
            pltpu.VMEM((ROUNDS, 8, 128), jnp.int32),
            pltpu.VMEM((2, COMP * 2 * SLOTS, CHUNK), bf16),
            pltpu.VMEM((ROUNDS, 2 * GROUP, 16, 128), bf16),
            pltpu.VMEM((ROUNDS, 2 * GROUP, 16, 128), bf16),
            dma((3,)),
            dma((ROUNDS, GROUP)),
            dma((ROUNDS, GROUP)),
            dma((ROUNDS,)),
            dma((ROUNDS,)),
            dma((ROUNDS, 2 * GROUP)),
            dma((ROUNDS, 2 * GROUP)),
            pltpu.SemaphoreType.REGULAR,
        ],
        compiler_params=pltpu.CompilerParams(
            collective_id=0, has_side_effects=True, vmem_limit_bytes=48 * 2**20
        ),
        name="correlate",
    )(
        jnp.transpose(waveforms, (0, 2, 1, 3)),
        jnp.transpose(pair_lists, (0, 2, 1)),
        jnp.asarray(forward),
        jnp.asarray(inverse),
    )
    slot = lax.axis_index("station") * 8 + jnp.arange(8, dtype=jnp.int32)
    live = slot[None, :] < pair_counts
    return jnp.where(live[:, :, None], curves, jnp.zeros_like(curves))


def solution(mesh):
    return jax.shard_map(
        shards,
        mesh=mesh,
        in_specs=(P("region", "station", None, None), P(None, "region", None), P(None, "region")),
        out_specs=P(None, ("region", "station"), None),
        check_vma=False,
    )
```

```python
import math

import jax
import jax.numpy as jnp
import numpy as np
from jax import lax
from jax.experimental import pallas as pl
from jax.experimental.pallas import tpu as pltpu
from jax.sharding import PartitionSpec as P

MESH = pl.DeviceIdType.MESH
ROUNDS = 3
EVENTS = 16
GROUP = 4
COMP = 3
LENGTH = 512
LAGS = 256
SLOTS = 32
STATIONS = 16
EPS = 1e-06
CHUNK = COMP * EVENTS
TRACES = GROUP * CHUNK
PERIOD = LENGTH + LAGS // 2
HALF = PERIOD // 2
WIDE = 3 * LAGS
GRANT = 60 * 2**20
HALVES = 2


def tables():
    order = np.arange(HALF)
    times = np.arange(LENGTH)[:, None]
    angle = 2.0 * np.pi * ((2 * order[None, :] + 1) * times % (2 * PERIOD)) / (2 * PERIOD)
    real, imag = np.cos(angle), -np.sin(angle)
    forward = np.concatenate([real[:, :256], imag[:, :256], real[:, 256:], imag[:, 256:]], axis=1)
    lags = np.arange(LAGS)[None, :] - LAGS // 2
    angle = 2.0 * np.pi * ((2 * order[:, None] + 1) * lags % (2 * PERIOD)) / (2 * PERIOD)
    factor = 2.0 / (PERIOD * math.sqrt(STATIONS * COMP * LENGTH))
    cos, sin = factor * np.cos(angle), factor * np.sin(angle)
    inverse = np.concatenate(
        [cos[:256], -sin[:256], cos[256:], cos[256:], -sin[256:], sin[256:]], axis=0
    )
    return forward.astype(jnp.bfloat16), inverse.astype(jnp.bfloat16)


def kernel(
    x_hbm, lists_ref, counts_ref, forward_hbm, inverse_hbm, out_ref,
    x_in, forward, inverse, normal, arrived, spectra, theirs, left, right, total,
    message, heard, picks, shares, gathered,
    load_sem, wave_out, wave_in, relay_out, list_out, list_in, share_out, share_in, near_ready, far_ready,
):
    region, group = lax.axis_index("region"), lax.axis_index("station")
    z = lax.rem(region, 8)
    bits = [lax.rem(z // (1 << e), 2) for e in range(ROUNDS)]
    step = [(1 << e) * (1 - 2 * bits[e]) for e in range(ROUNDS)]
    partner = [region + step[e] for e in range(ROUNDS)]
    onward = [region + step[0] + step[1], region + step[1] + step[2]]
    mates = [lax.rem(group + d, GROUP) for d in range(GROUP)]
    late = bits[2]
    middle = lax.rem(bits[0] + bits[1], 2)
    odd = lax.rem(bits[0] + bits[1] + bits[2], 2)
    worked, sent = odd * HALVES * CHUNK, (1 - odd) * HALVES * CHUNK

    barrier = pltpu.get_barrier_semaphore()

    def greet(which, to):
        pl.semaphore_signal(which, inc=1, device_id=to, device_id_type=MESH)

    for e in range(2):
        for d in range(GROUP):
            greet(barrier, (partner[e], mates[d]))
    for d in range(1, GROUP):
        greet(barrier, (region, mates[d]))

    @pl.when(middle == 1)
    def _():
        greet(barrier, (onward[0], group))

    @pl.when(late == 0)
    def _():
        greet(barrier, (onward[1], group))
        for d in range(GROUP):
            greet(barrier, (partner[2], mates[d]))

    loads = [
        pltpu.make_async_copy(x_hbm, x_in, load_sem.at[0]),
        pltpu.make_async_copy(forward_hbm, forward, load_sem.at[1]),
        pltpu.make_async_copy(inverse_hbm, inverse, load_sem.at[2]),
    ]
    for load in loads:
        load.start()

    message[...] = jnp.zeros_like(message)
    for e in range(ROUNDS):
        message[2 * e : 2 * e + 2, 0:SLOTS] = lists_ref[e]
    mine = message[...]
    turned = pltpu.roll(mine, SLOTS, 1)
    even = lax.rem(lax.broadcasted_iota(jnp.int32, (8, 128), 0), 2) == 0
    turned = jnp.where(even, pltpu.roll(turned, 7, 0), pltpu.roll(turned, 1, 0))
    message[...] = turned

    loads[0].wait()
    traces = x_in[...].astype(jnp.float32).reshape(TRACES, LENGTH)
    traces = traces - jnp.mean(traces, axis=-1, keepdims=True)
    traces = traces * lax.rsqrt(jnp.mean(traces * traces, axis=-1, keepdims=True) + EPS)
    row = lax.broadcasted_iota(jnp.int32, (TRACES, TRACES), 0)
    column = lax.broadcasted_iota(jnp.int32, (TRACES, TRACES), 1)
    source = lax.rem(row, EVENTS) * (COMP * GROUP) + lax.rem(row // EVENTS, COMP) * GROUP + row // CHUNK
    reorder = jnp.where(column == source, 1.0, 0.0).astype(jnp.bfloat16)
    normal[...] = jnp.dot(
        reorder, traces.astype(jnp.bfloat16), preferred_element_type=jnp.float32
    ).astype(jnp.bfloat16)

    def rows(base, h):
        return pl.ds(pl.multiple_of(base + h * CHUNK, CHUNK), CHUNK)

    def wave(e, h):
        return pltpu.make_async_remote_copy(
            src_ref=normal.at[rows(sent, h)],
            dst_ref=arrived.at[e, rows(0, h)],
            send_sem=wave_out.at[e, h],
            recv_sem=wave_in.at[e, h],
            device_id=(partner[e], group),
            device_id_type=MESH,
        )

    def relay(e, h):
        return pltpu.make_async_remote_copy(
            src_ref=arrived.at[e, rows(0, h)],
            dst_ref=arrived.at[e + 1, rows(0, h)],
            send_sem=relay_out.at[e, h],
            recv_sem=wave_in.at[e + 1, h],
            device_id=(onward[e], group),
            device_id_type=MESH,
        )

    def listing(e):
        return pltpu.make_async_remote_copy(
            src_ref=message if e < 2 else heard.at[1],
            dst_ref=heard.at[e],
            send_sem=list_out.at[e],
            recv_sem=list_in.at[e],
            device_id=(partner[e] if e < 2 else onward[1], group),
            device_id_type=MESH,
        )

    def share(e, side, d):
        to = region if side == 0 else partner[e]
        return pltpu.make_async_remote_copy(
            src_ref=shares.at[e, GROUP * side + mates[d]],
            dst_ref=gathered.at[e, GROUP * side + group],
            send_sem=share_out.at[e, GROUP * side + mates[d]],
            recv_sem=share_in.at[e, GROUP * side + group],
            device_id=(to, mates[d]),
            device_id_type=MESH,
        )

    def landed(e, side, d):
        to = region if side == 0 else partner[e]
        return pltpu.make_async_remote_copy(
            src_ref=shares.at[e, GROUP * side + mates[d]],
            dst_ref=gathered.at[e, GROUP * side + mates[d]],
            send_sem=share_out.at[e, GROUP * side + mates[d]],
            recv_sem=share_in.at[e, GROUP * side + mates[d]],
            device_id=(to, mates[d]),
            device_id_type=MESH,
        )

    @pl.when(late == 0)
    def _():
        pl.semaphore_wait(barrier, 11 + middle)

    @pl.when(late == 1)
    def _():
        pl.semaphore_wait(barrier, 16 + middle)
        greet(near_ready, (onward[1], group))
        for d in range(GROUP):
            greet(far_ready, (partner[2], mates[d]))

    for h in range(HALVES):
        wave(0, h).start()

        @pl.when(middle == 1)
        def _(h=h):
            wave(1, h).start()

    for e in range(2):
        listing(e).start()

    loads[1].wait()
    spectra[...] = jnp.dot(
        normal[pl.ds(pl.multiple_of(worked, CHUNK), HALVES * CHUNK)], forward[...], preferred_element_type=jnp.float32
    ).astype(jnp.bfloat16)
    loads[2].wait()

    lane = lax.broadcasted_iota(jnp.int32, (8, 128), 1)
    cell = lax.broadcasted_iota(jnp.int32, (COMP * 2 * SLOTS, CHUNK), 1)
    part = lax.broadcasted_iota(jnp.int32, (COMP * 2 * SLOTS, CHUNK), 0) // (2 * SLOTS) * EVENTS
    theirs_row = lax.broadcasted_iota(jnp.int32, (2 * SLOTS, LAGS), 0) >= SLOTS

    def work(e):
        events = jnp.where(lane < SLOTS, mine, heard[e]).astype(jnp.float32).T
        for side in range(2):
            event = events[: 2 * SLOTS, 2 * e + side : 2 * e + side + 1].astype(jnp.int32)
            event = jnp.concatenate([event] * COMP, axis=0)
            picks[side] = jnp.where(cell == part + event, 1.0, 0.0).astype(jnp.bfloat16)
        total[...] = jnp.zeros_like(total)

        @pl.loop(0, HALVES)
        def _(h):
            if e == 2:
                wave(e, h).wait_recv()
            theirs[...] = jnp.dot(
                arrived[e, rows(0, h)], forward[...], preferred_element_type=jnp.float32
            ).astype(jnp.bfloat16)
            left[...] = jnp.dot(picks[0], spectra[rows(0, h)], preferred_element_type=jnp.float32)
            right[...] = jnp.dot(picks[1], theirs[...], preferred_element_type=jnp.float32)
            for c in range(COMP):
                at = pl.ds(c * 2 * SLOTS, 2 * SLOTS)
                lr, li, lm = left[at, 0:256], left[at, 256:512], left[at, 512:640]
                rr, ri, rm = right[at, 0:256], right[at, 256:512], right[at, 512:640]
                total[:, 0:256] += lr * rr + li * ri
                total[:, 256:512] += lr * ri - li * rr
                total[:, 512:640] += lm * rm
                total[:, 640:768] += lm * pltpu.roll(rm, 64, 1)

        real, imag, both, cross = total[:, 0:256], total[:, 256:512], total[:, 512:640], total[:, 640:768]
        imag = jnp.where(theirs_row, -imag, imag)
        cross = jnp.where(theirs_row[:, :128], -cross, cross)
        curves = jnp.dot(
            jnp.concatenate([real, imag, both, cross], axis=1).astype(jnp.bfloat16),
            inverse[...],
            preferred_element_type=jnp.float32,
        )
        for k in range(2 * GROUP):
            piece = curves[8 * k : 8 * k + 8]
            shares[e, k] = jnp.concatenate([piece[:, :128], piece[:, 128:]], axis=0).astype(jnp.bfloat16)
        if e == 2:

            @pl.when(late == 0)
            def _():
                pl.semaphore_wait(far_ready, GROUP)

        for d in range(GROUP):
            share(e, 1, d).start()
        for d in range(1, GROUP):
            share(e, 0, d).start()
        gathered[e, pl.ds(group, 1)] = shares[e, pl.ds(group, 1)]

    for h in range(HALVES):
        wave(0, h).wait_recv()

        @pl.when(middle == 1)
        def _(h=h):
            relay(0, h).start()

    for h in range(HALVES):
        wave(1, h).wait_recv()
        if h == 0:

            @pl.when(late == 0)
            def _():
                pl.semaphore_wait(near_ready, 1)

        relay(1, h).start()
    listing(1).wait_recv()
    listing(2).start()
    listing(0).wait_recv()
    work(0)
    work(1)
    listing(2).wait_recv()
    work(2)

    slot = group * 8 + lax.rem(lax.broadcasted_iota(jnp.int32, (16, 128), 0), 8)
    for e in range(ROUNDS):
        for d in range(1, GROUP):
            landed(e, 0, d).wait_recv()
        for d in range(GROUP):
            landed(e, 1, d).wait_recv()
        curve = jnp.sum(gathered[e].astype(jnp.float32), axis=0)
        curve = jnp.where(slot < counts_ref[0, e], curve, 0.0)
        out_ref[e, :, 0:128] = curve[0:8]
        out_ref[e, :, 128:256] = curve[8:16]

    for h in range(HALVES):
        wave(0, h).wait_send()
        relay(1, h).wait_send()

        @pl.when(middle == 1)
        def _(h=h):
            wave(1, h).wait_send()
            relay(0, h).wait_send()

    for e in range(ROUNDS):
        listing(e).wait_send()
        for d in range(1, GROUP):
            share(e, 0, d).wait_send()
        for d in range(GROUP):
            share(e, 1, d).wait_send()


def shards(waveforms, pair_lists, pair_counts):
    forward, inverse = tables()
    bf16, f32 = jnp.bfloat16, jnp.float32
    dma = pltpu.SemaphoreType.DMA
    return pl.pallas_call(
        kernel,
        out_shape=jax.ShapeDtypeStruct((ROUNDS, 8, LAGS), f32),
        in_specs=[
            pl.BlockSpec(memory_space=pltpu.HBM),
            pl.BlockSpec(memory_space=pltpu.VMEM),
            pl.BlockSpec(memory_space=pltpu.SMEM),
            pl.BlockSpec(memory_space=pltpu.HBM),
            pl.BlockSpec(memory_space=pltpu.HBM),
        ],
        out_specs=pl.BlockSpec(memory_space=pltpu.VMEM),
        scratch_shapes=[
            pltpu.VMEM((EVENTS, COMP, GROUP, LENGTH), bf16),
            pltpu.VMEM((LENGTH, PERIOD), bf16),
            pltpu.VMEM((WIDE, LAGS), bf16),
            pltpu.VMEM((TRACES, LENGTH), bf16),
            pltpu.VMEM((ROUNDS, HALVES * CHUNK, LENGTH), bf16),
            pltpu.VMEM((HALVES * CHUNK, PERIOD), bf16),
            pltpu.VMEM((CHUNK, PERIOD), bf16),
            pltpu.VMEM((COMP * 2 * SLOTS, PERIOD), f32),
            pltpu.VMEM((COMP * 2 * SLOTS, PERIOD), f32),
            pltpu.VMEM((2 * SLOTS, WIDE), f32),
            pltpu.VMEM((8, 128), jnp.int32),
            pltpu.VMEM((ROUNDS, 8, 128), jnp.int32),
            pltpu.VMEM((2, COMP * 2 * SLOTS, CHUNK), bf16),
            pltpu.VMEM((ROUNDS, 2 * GROUP, 16, 128), bf16),
            pltpu.VMEM((ROUNDS, 2 * GROUP, 16, 128), bf16),
            dma((3,)),
            dma((2, HALVES)),
            dma((ROUNDS, HALVES)),
            dma((2, HALVES)),
            dma((ROUNDS,)),
            dma((ROUNDS,)),
            dma((ROUNDS, 2 * GROUP)),
            dma((ROUNDS, 2 * GROUP)),
            pltpu.SemaphoreType.REGULAR,
            pltpu.SemaphoreType.REGULAR,
        ],
        compiler_params=pltpu.CompilerParams(
            collective_id=0, has_side_effects=True, vmem_limit_bytes=GRANT
        ),
        name="correlate",
    )(
        jnp.transpose(waveforms, (0, 2, 1, 3)),
        jnp.transpose(pair_lists, (0, 2, 1)),
        jnp.transpose(pair_counts, (1, 0)),
        jnp.asarray(forward),
        jnp.asarray(inverse),
    )


def solution(mesh):
    return jax.shard_map(
        shards,
        mesh=mesh,
        in_specs=(P("region", "station", None, None), P(None, "region", None), P(None, "region")),
        out_specs=P(None, ("region", "station"), None),
        check_vma=False,
    )
```

```python
import math

import jax
import jax.numpy as jnp
import numpy as np
from jax import lax
from jax.experimental import pallas as pl
from jax.experimental.pallas import tpu as pltpu
from jax.sharding import PartitionSpec as P

MESH = pl.DeviceIdType.MESH
ROUNDS = 3
EVENTS = 16
GROUP = 4
COMP = 3
LENGTH = 512
LAGS = 256
SLOTS = 32
STATIONS = 16
EPS = 1e-06
CHUNK = COMP * EVENTS
TRACES = GROUP * CHUNK
PERIOD = LENGTH + LAGS // 2
HALF = PERIOD // 2
WIDE = 3 * LAGS
GRANT = 55200 * 2**10
HALVES = 2


def tables():
    order = np.arange(HALF)
    times = np.arange(LENGTH)[:, None]
    angle = 2.0 * np.pi * ((2 * order[None, :] + 1) * times % (2 * PERIOD)) / (2 * PERIOD)
    real, imag = np.cos(angle), -np.sin(angle)
    forward = np.concatenate([real[:, :256], imag[:, :256], real[:, 256:], imag[:, 256:]], axis=1)
    lags = np.arange(LAGS)[None, :] - LAGS // 2
    angle = 2.0 * np.pi * ((2 * order[:, None] + 1) * lags % (2 * PERIOD)) / (2 * PERIOD)
    factor = 2.0 / (PERIOD * math.sqrt(STATIONS * COMP * LENGTH))
    cos, sin = factor * np.cos(angle), factor * np.sin(angle)
    inverse = np.concatenate(
        [cos[:256], -sin[:256], cos[256:], cos[256:], -sin[256:], sin[256:]], axis=0
    )
    return forward.astype(jnp.bfloat16), inverse.astype(jnp.bfloat16)


def kernel(
    x_hbm, lists_hbm, counts_hbm, forward_hbm, inverse_hbm, out_ref,
    x_in, lists_ref, counts_ref, forward, inverse, normal, arrived, spectra, left, right, total,
    message, heard, picks, shares, gathered,
    load_sem, wave_out, wave_in, list_out, list_in, share_out, share_in, ready, settled,
):
    region, group = lax.axis_index("region"), lax.axis_index("station")
    z = lax.rem(region, 8)
    bits = [lax.rem(z // (1 << e), 2) for e in range(ROUNDS)]
    step = [(1 << e) * (1 - 2 * bits[e]) for e in range(ROUNDS)]
    partner = [region + step[0], region + step[1], region + step[1] + step[2]]
    mates = [lax.rem(group + d, GROUP) for d in range(GROUP)]
    late = bits[2]
    odd = lax.rem(bits[0] + bits[1] + bits[2], 2)
    worked, sent = odd * HALVES * CHUNK, (1 - odd) * HALVES * CHUNK

    barrier = pltpu.get_barrier_semaphore()

    def greet(which, to):
        pl.semaphore_signal(which, inc=1, device_id=to, device_id_type=MESH)

    greet(barrier, (partner[1], group))
    greet(barrier, (partner[0], group))
    for d in range(1, GROUP):
        greet(barrier, (region, mates[d]))

    @pl.when(late == 0)
    def _():
        greet(barrier, (partner[2], group))

    loads = [
        pltpu.make_async_copy(x_hbm, x_in, load_sem.at[0]),
        pltpu.make_async_copy(forward_hbm, forward, load_sem.at[1]),
        pltpu.make_async_copy(inverse_hbm, inverse, load_sem.at[2]),
        pltpu.make_async_copy(lists_hbm, lists_ref, load_sem.at[3]),
        pltpu.make_async_copy(counts_hbm, counts_ref, load_sem.at[4]),
    ]
    for load in loads:
        load.start()

    loads[3].wait()
    message[...] = jnp.zeros_like(message)
    for e in range(ROUNDS):
        message[2 * e : 2 * e + 2, 0:SLOTS] = lists_ref[e]
    mine = message[...]
    turned = pltpu.roll(mine, SLOTS, 1)
    even = lax.rem(lax.broadcasted_iota(jnp.int32, (8, 128), 0), 2) == 0
    turned = jnp.where(even, pltpu.roll(turned, 7, 0), pltpu.roll(turned, 1, 0))
    message[...] = mine + turned

    loads[0].wait()
    traces = x_in[...].astype(jnp.float32).reshape(TRACES, LENGTH)
    traces = traces - jnp.mean(traces, axis=-1, keepdims=True)
    traces = traces * lax.rsqrt(jnp.mean(traces * traces, axis=-1, keepdims=True) + EPS)
    row = lax.broadcasted_iota(jnp.int32, (TRACES, TRACES), 0)
    column = lax.broadcasted_iota(jnp.int32, (TRACES, TRACES), 1)
    source = lax.rem(row, EVENTS) * (COMP * GROUP) + lax.rem(row // EVENTS, COMP) * GROUP + row // CHUNK
    reorder = jnp.where(column == source, 1.0, 0.0).astype(jnp.bfloat16)
    normal[...] = jnp.dot(
        reorder, traces.astype(jnp.bfloat16), preferred_element_type=jnp.float32
    ).astype(jnp.bfloat16)

    def rows(base, h):
        return pl.ds(pl.multiple_of(base + h * CHUNK, CHUNK), CHUNK)

    def wave(e, h):
        return pltpu.make_async_remote_copy(
            src_ref=normal.at[rows(sent if e < 2 else worked, h)],
            dst_ref=arrived.at[e, rows(0, h)],
            send_sem=wave_out.at[e, h],
            recv_sem=wave_in.at[e, h],
            device_id=(partner[e], group),
            device_id_type=MESH,
        )

    def listing(e):
        return pltpu.make_async_remote_copy(
            src_ref=message,
            dst_ref=heard.at[e],
            send_sem=list_out.at[e],
            recv_sem=list_in.at[e],
            device_id=(partner[e], group),
            device_id_type=MESH,
        )

    def share(e, side, d):
        to = partner[e] if side == 1 else partner[1] if e == 2 else region
        return pltpu.make_async_remote_copy(
            src_ref=shares.at[e, GROUP * side + mates[d]],
            dst_ref=gathered.at[e, GROUP * side + group],
            send_sem=share_out.at[e, GROUP * side + mates[d]],
            recv_sem=share_in.at[e, GROUP * side + group],
            device_id=(to, mates[d]),
            device_id_type=MESH,
        )

    def landed(e, side, d):
        to = partner[e] if side == 1 else partner[1] if e == 2 else region
        return pltpu.make_async_remote_copy(
            src_ref=shares.at[e, GROUP * side + mates[d]],
            dst_ref=gathered.at[e, GROUP * side + mates[d]],
            send_sem=share_out.at[e, GROUP * side + mates[d]],
            recv_sem=share_in.at[e, GROUP * side + mates[d]],
            device_id=(to, mates[d]),
            device_id_type=MESH,
        )

    def send(e):
        for h in range(HALVES):
            wave(e, h).start()
        listing(e).start()

    @pl.when(late == 0)
    def _():
        pl.semaphore_wait(barrier, 5)

    @pl.when(late == 1)
    def _():
        pl.semaphore_wait(barrier, 6)
        greet(ready, (partner[2], group))
        send(2)

    send(1)
    send(0)

    loads[1].wait()
    spectra[0] = jnp.dot(
        normal[pl.ds(pl.multiple_of(worked, CHUNK), HALVES * CHUNK)], forward[...], preferred_element_type=jnp.float32
    ).astype(jnp.bfloat16)
    loads[2].wait()
    loads[4].wait()

    @pl.when(late == 0)
    def _():
        pl.semaphore_wait(ready, 1)
        send(2)

    for d in range(1, GROUP):
        greet(settled, (region, mates[d]))

    lane = lax.broadcasted_iota(jnp.int32, (8, 128), 1)
    cell = lax.broadcasted_iota(jnp.int32, (COMP * 2 * SLOTS, CHUNK), 1)
    part = lax.broadcasted_iota(jnp.int32, (COMP * 2 * SLOTS, CHUNK), 0) // (2 * SLOTS) * EVENTS
    theirs_row = lax.broadcasted_iota(jnp.int32, (2 * SLOTS, LAGS), 0) >= SLOTS

    def work(e):
        listing(e).wait_recv()
        events = jnp.where(lane < SLOTS, heard[1] if e == 2 else message[...], heard[e]).astype(jnp.float32).T
        for side in range(2):
            event = events[: 2 * SLOTS, 2 * e + side : 2 * e + side + 1].astype(jnp.int32)
            event = jnp.concatenate([event] * COMP, axis=0)
            picks[side] = jnp.where(cell == part + event, 1.0, 0.0).astype(jnp.bfloat16)
        total[...] = jnp.zeros_like(total)

        @pl.loop(0, HALVES)
        def _(h):
            wave(e, h).wait_recv()
            spectra[1 + e, rows(0, h)] = jnp.dot(
                arrived[e, rows(0, h)], forward[...], preferred_element_type=jnp.float32
            ).astype(jnp.bfloat16)
            left[...] = jnp.dot(picks[0], spectra[e if e == 2 else 0, rows(0, h)], preferred_element_type=jnp.float32)
            right[...] = jnp.dot(picks[1], spectra[1 + e, rows(0, h)], preferred_element_type=jnp.float32)
            for c in range(COMP):
                at = pl.ds(c * 2 * SLOTS, 2 * SLOTS)
                lr, li, lm = left[at, 0:256], left[at, 256:512], left[at, 512:640]
                rr, ri, rm = right[at, 0:256], right[at, 256:512], right[at, 512:640]
                total[:, 0:256] += lr * rr + li * ri
                total[:, 256:512] += lr * ri - li * rr
                total[:, 512:640] += lm * rm
                total[:, 640:768] += lm * pltpu.roll(rm, 64, 1)

        real, imag, both, cross = total[:, 0:256], total[:, 256:512], total[:, 512:640], total[:, 640:768]
        imag = jnp.where(theirs_row, -imag, imag)
        cross = jnp.where(theirs_row[:, :128], -cross, cross)
        curves = jnp.dot(
            jnp.concatenate([real, imag, both, cross], axis=1).astype(jnp.bfloat16),
            inverse[...],
            preferred_element_type=jnp.float32,
        )
        for k in range(2 * GROUP):
            piece = curves[8 * k : 8 * k + 8]
            shares[e, k] = jnp.concatenate([piece[:, :128], piece[:, 128:]], axis=0).astype(jnp.bfloat16)
        for side in range(2):
            for d in range(GROUP):
                if e == 2 or side == 1 or d > 0:
                    share(e, side, d).start()
        if e < 2:
            gathered[e, pl.ds(group, 1)] = shares[e, pl.ds(group, 1)]

    pl.semaphore_wait(settled, GROUP - 1)
    work(1)

    @pl.when(late == 0)
    def _():
        work(0)

    work(2)

    @pl.when(late == 1)
    def _():
        work(0)

    slot = group * 8 + lax.rem(lax.broadcasted_iota(jnp.int32, (16, 128), 0), 8)
    for e in range(ROUNDS):
        for side in range(2):
            for d in range(GROUP):
                if e == 2 or side == 1 or d > 0:
                    landed(e, side, d).wait_recv()
        curve = jnp.sum(gathered[e].astype(jnp.float32), axis=0)
        curve = jnp.where(slot < counts_ref[0, e], curve, 0.0)
        out_ref[e, :, 0:128] = curve[0:8]
        out_ref[e, :, 128:256] = curve[8:16]

    for e in range(ROUNDS):
        listing(e).wait_send()
        for h in range(HALVES):
            wave(e, h).wait_send()
        for side in range(2):
            for d in range(GROUP):
                if e == 2 or side == 1 or d > 0:
                    share(e, side, d).wait_send()


def shards(waveforms, pair_lists, pair_counts):
    forward, inverse = tables()
    bf16, f32 = jnp.bfloat16, jnp.float32
    dma = pltpu.SemaphoreType.DMA
    return pl.pallas_call(
        kernel,
        out_shape=jax.ShapeDtypeStruct((ROUNDS, 8, LAGS), f32),
        in_specs=[
            pl.BlockSpec(memory_space=pl.ANY),
            pl.BlockSpec(memory_space=pl.ANY),
            pl.BlockSpec(memory_space=pl.ANY),
            pl.BlockSpec(memory_space=pl.ANY),
            pl.BlockSpec(memory_space=pl.ANY),
        ],
        out_specs=pl.BlockSpec(memory_space=pltpu.VMEM),
        scratch_shapes=[
            pltpu.VMEM((EVENTS, COMP, GROUP, LENGTH), bf16),
            pltpu.VMEM((ROUNDS, 2, SLOTS), jnp.int32),
            pltpu.SMEM((1, ROUNDS), jnp.int32),
            pltpu.VMEM((LENGTH, PERIOD), bf16),
            pltpu.VMEM((WIDE, LAGS), bf16),
            pltpu.VMEM((TRACES, LENGTH), bf16),
            pltpu.VMEM((ROUNDS, HALVES * CHUNK, LENGTH), bf16),
            pltpu.VMEM((1 + ROUNDS, HALVES * CHUNK, PERIOD), bf16),
            pltpu.VMEM((COMP * 2 * SLOTS, PERIOD), f32),
            pltpu.VMEM((COMP * 2 * SLOTS, PERIOD), f32),
            pltpu.VMEM((2 * SLOTS, WIDE), f32),
            pltpu.VMEM((8, 128), jnp.int32),
            pltpu.VMEM((ROUNDS, 8, 128), jnp.int32),
            pltpu.VMEM((2, COMP * 2 * SLOTS, CHUNK), bf16),
            pltpu.VMEM((ROUNDS, 2 * GROUP, 16, 128), bf16),
            pltpu.VMEM((ROUNDS, 2 * GROUP, 16, 128), bf16),
            dma((5,)),
            dma((ROUNDS, HALVES)),
            dma((ROUNDS, HALVES)),
            dma((ROUNDS,)),
            dma((ROUNDS,)),
            dma((ROUNDS, 2 * GROUP)),
            dma((ROUNDS, 2 * GROUP)),
            pltpu.SemaphoreType.REGULAR,
            pltpu.SemaphoreType.REGULAR,
        ],
        compiler_params=pltpu.CompilerParams(
            collective_id=0, has_side_effects=True, vmem_limit_bytes=GRANT
        ),
        name="correlate",
    )(
        jnp.transpose(waveforms, (0, 2, 1, 3)),
        jnp.transpose(pair_lists, (0, 2, 1)),
        jnp.transpose(pair_counts, (1, 0)),
        jnp.asarray(forward),
        jnp.asarray(inverse),
    )


def solution(mesh):
    return jax.shard_map(
        shards,
        mesh=mesh,
        in_specs=(P("region", "station", None, None), P(None, "region", None), P(None, "region")),
        out_specs=P(None, ("region", "station"), None),
        check_vma=False,
    )
```

```python
import math

import jax
import jax.numpy as jnp
import numpy as np
from jax import lax
from jax.experimental import pallas as pl
from jax.experimental.pallas import tpu as pltpu
from jax.sharding import PartitionSpec as P

MESH = pl.DeviceIdType.MESH
ROUNDS = 3
EVENTS = 16
GROUP = 4
COMP = 3
LENGTH = 512
LAGS = 256
SLOTS = 32
STATIONS = 16
EPS = 1e-06
CHUNK = COMP * EVENTS
TRACES = GROUP * CHUNK
PERIOD = LENGTH + LAGS // 2
HALF = PERIOD // 2
WIDE = 3 * LAGS
GRANT = 55200 * 2**10
HALVES = 2
SHIFT = 2
LEFT_OUT = SHIFT * EVENTS


def tables():
    order = np.arange(HALF)
    times = np.arange(LENGTH)[:, None]
    angle = 2.0 * np.pi * ((2 * order[None, :] + 1) * times % (2 * PERIOD)) / (2 * PERIOD)
    real, imag = np.cos(angle), -np.sin(angle)
    forward = np.concatenate([real[:, :256], imag[:, :256], real[:, 256:], imag[:, 256:]], axis=1)
    lags = np.arange(LAGS)[None, :] - LAGS // 2
    angle = 2.0 * np.pi * ((2 * order[:, None] + 1) * lags % (2 * PERIOD)) / (2 * PERIOD)
    factor = 2.0 / (PERIOD * math.sqrt(STATIONS * COMP * LENGTH))
    cos, sin = factor * np.cos(angle), factor * np.sin(angle)
    inverse = np.concatenate(
        [cos[:256], -sin[:256], cos[256:], cos[256:], -sin[256:], sin[256:]], axis=0
    )
    return forward.astype(jnp.bfloat16), inverse.astype(jnp.bfloat16)


def kernel(
    x_hbm, lists_hbm, counts_hbm, forward_hbm, inverse_hbm, out_ref,
    x_in, lists_ref, counts_ref, forward, inverse, normal, arrived, spectra, left, right, total,
    message, heard, picks, shares, gathered,
    load_sem, wave_out, wave_in, list_out, list_in, share_out, share_in, ready, settled,
):
    region, group = lax.axis_index("region"), lax.axis_index("station")
    z = lax.rem(region, 8)
    bits = [lax.rem(z // (1 << e), 2) for e in range(ROUNDS)]
    step = [(1 << e) * (1 - 2 * bits[e]) for e in range(ROUNDS)]
    partner = [region + step[0], region + step[1], region + step[1] + step[2]]
    mates = [lax.rem(group + d, GROUP) for d in range(GROUP)]
    late = bits[2]
    odd = lax.rem(bits[0] + bits[1] + bits[2], 2)
    worked, sent = odd * HALVES * CHUNK, (1 - odd) * HALVES * CHUNK

    arrived[1, HALVES * CHUNK :] = jnp.zeros_like(arrived[1, HALVES * CHUNK :])
    arrived[2, HALVES * CHUNK - LEFT_OUT :] = jnp.zeros_like(arrived[2, HALVES * CHUNK - LEFT_OUT :])
    barrier = pltpu.get_barrier_semaphore()

    def greet(which, to):
        pl.semaphore_signal(which, inc=1, device_id=to, device_id_type=MESH)

    greet(barrier, (partner[1], group))
    greet(barrier, (partner[0], group))
    for d in range(1, GROUP):
        greet(barrier, (region, mates[d]))

    @pl.when(late == 0)
    def _():
        greet(barrier, (partner[2], group))

    loads = [
        pltpu.make_async_copy(x_hbm, x_in, load_sem.at[0]),
        pltpu.make_async_copy(forward_hbm, forward, load_sem.at[1]),
        pltpu.make_async_copy(inverse_hbm, inverse, load_sem.at[2]),
        pltpu.make_async_copy(lists_hbm, lists_ref, load_sem.at[3]),
        pltpu.make_async_copy(counts_hbm, counts_ref, load_sem.at[4]),
    ]
    for load in loads:
        load.start()

    loads[3].wait()
    message[...] = jnp.zeros_like(message)
    for e in range(ROUNDS):
        message[2 * e : 2 * e + 2, 0:SLOTS] = lists_ref[e]
    mine = message[...]
    turned = pltpu.roll(mine, SLOTS, 1)
    even = lax.rem(lax.broadcasted_iota(jnp.int32, (8, 128), 0), 2) == 0
    turned = jnp.where(even, pltpu.roll(turned, 7, 0), pltpu.roll(turned, 1, 0))
    message[...] = mine + turned

    loads[0].wait()
    traces = x_in[...].astype(jnp.float32).reshape(TRACES, LENGTH)
    traces = traces - jnp.mean(traces, axis=-1, keepdims=True)
    traces = traces * lax.rsqrt(jnp.mean(traces * traces, axis=-1, keepdims=True) + EPS)
    row = lax.broadcasted_iota(jnp.int32, (TRACES, TRACES), 0)
    column = lax.broadcasted_iota(jnp.int32, (TRACES, TRACES), 1)
    source = lax.rem(row, EVENTS) * (COMP * GROUP) + lax.rem(row // EVENTS, COMP) * GROUP + row // CHUNK
    reorder = jnp.where(column == source, 1.0, 0.0).astype(jnp.bfloat16)
    normal[...] = jnp.dot(
        reorder, traces.astype(jnp.bfloat16), preferred_element_type=jnp.float32
    ).astype(jnp.bfloat16)

    def rows(base, h):
        return pl.ds(pl.multiple_of(base + h * CHUNK, CHUNK), CHUNK)

    def copy(e, h, src, dst, size):
        return pltpu.make_async_remote_copy(
            src_ref=normal.at[pl.ds(pl.multiple_of(src, EVENTS), size)],
            dst_ref=arrived.at[e, pl.ds(dst, size)],
            send_sem=wave_out.at[e, h],
            recv_sem=wave_in.at[e, h],
            device_id=(partner[e], group),
            device_id_type=MESH,
        )

    last = HALVES * CHUNK - LEFT_OUT

    def wave(e, h):
        if e < 2:
            if h < HALVES:
                return copy(e, h, sent + h * CHUNK, h * CHUNK, CHUNK)
            return copy(e, h, worked + last, last + CHUNK, LEFT_OUT)
        if h == 0:
            return copy(e, h, worked, 0, CHUNK)
        if h == 1:
            return copy(e, h, worked + CHUNK, CHUNK, CHUNK - LEFT_OUT)
        if h == 2:
            return copy(e, h, worked + last, last, LEFT_OUT)
        return copy(e, h, sent + last, last + CHUNK, LEFT_OUT)

    def listing(e):
        return pltpu.make_async_remote_copy(
            src_ref=message,
            dst_ref=heard.at[e],
            send_sem=list_out.at[e],
            recv_sem=list_in.at[e],
            device_id=(partner[e], group),
            device_id_type=MESH,
        )

    def share(e, side, d):
        to = partner[e] if side == 1 else partner[1] if e == 2 else region
        return pltpu.make_async_remote_copy(
            src_ref=shares.at[e, GROUP * side + mates[d]],
            dst_ref=gathered.at[e, GROUP * side + group],
            send_sem=share_out.at[e, GROUP * side + mates[d]],
            recv_sem=share_in.at[e, GROUP * side + group],
            device_id=(to, mates[d]),
            device_id_type=MESH,
        )

    def landed(e, side, d):
        to = partner[e] if side == 1 else partner[1] if e == 2 else region
        return pltpu.make_async_remote_copy(
            src_ref=shares.at[e, GROUP * side + mates[d]],
            dst_ref=gathered.at[e, GROUP * side + mates[d]],
            send_sem=share_out.at[e, GROUP * side + mates[d]],
            recv_sem=share_in.at[e, GROUP * side + mates[d]],
            device_id=(to, mates[d]),
            device_id_type=MESH,
        )

    def send(e):
        listing(e).start()
        for h in range(HALVES):
            wave(e, h).start()

    @pl.when(late == 0)
    def _():
        pl.semaphore_wait(barrier, 5)

    @pl.when(late == 1)
    def _():
        pl.semaphore_wait(barrier, 6)
        greet(ready, (partner[2], group))
        send(2)
        wave(2, 2).start()
        wave(2, 3).start()

    send(1)
    send(0)

    @pl.when(late == 0)
    def _():
        wave(1, 2).start()

    loads[1].wait()
    spectra[0, : HALVES * CHUNK] = jnp.dot(
        normal[pl.ds(pl.multiple_of(worked, CHUNK), HALVES * CHUNK)], forward[...], preferred_element_type=jnp.float32
    ).astype(jnp.bfloat16)
    loads[2].wait()
    loads[4].wait()

    @pl.when(late == 0)
    def _():
        pl.semaphore_wait(ready, 1)
        send(2)

    for d in range(1, GROUP):
        greet(settled, (region, mates[d]))

    lane = lax.broadcasted_iota(jnp.int32, (8, 128), 1)
    cell = lax.broadcasted_iota(jnp.int32, (COMP * 2 * SLOTS, CHUNK), 1)
    part = lax.broadcasted_iota(jnp.int32, (COMP * 2 * SLOTS, CHUNK), 0) // (2 * SLOTS) * EVENTS
    theirs_row = lax.broadcasted_iota(jnp.int32, (2 * SLOTS, LAGS), 0) >= SLOTS

    def work(e):
        listing(e).wait_recv()
        events = jnp.where(lane < SLOTS, heard[1] if e == 2 else message[...], heard[e]).astype(jnp.float32).T
        for side in range(2):
            event = events[: 2 * SLOTS, 2 * e + side : 2 * e + side + 1].astype(jnp.int32)
            event = jnp.concatenate([event] * COMP, axis=0)
            picks[side] = jnp.where(cell == part + event, 1.0, 0.0).astype(jnp.bfloat16)
        total[...] = jnp.zeros_like(total)
        known = 2 if e == 2 else 0

        def pick_left(h):
            left[h] = jnp.dot(picks[0], spectra[known, h * CHUNK : (h + 1) * CHUNK], preferred_element_type=jnp.float32)

        for h in range(HALVES):
            pick_left(h)
        if e == 2:

            @pl.when(late == 0)
            def _():
                wave(1, 2).wait_recv()
                spectra[2, HALVES * CHUNK :] = jnp.dot(
                    arrived[1, HALVES * CHUNK :], forward[...], preferred_element_type=jnp.float32
                ).astype(jnp.bfloat16)
                pick_left(2)

        @pl.loop(0, HALVES + 1 - late if e == 2 else HALVES)
        def _(h):
            for k in range(HALVES):

                @pl.when(h == k)
                def _(k=k):
                    wave(e, k).wait_recv()

            if e == 2:
                for k in range(HALVES):

                    @pl.when((late == 0) & (h == k + 1))
                    def _(k=k):
                        wave(2, k + 2).wait_recv()

            spectra[1 + e, rows(0, h)] = jnp.dot(
                arrived[e, rows(0, h)], forward[...], preferred_element_type=jnp.float32
            ).astype(jnp.bfloat16)
            right[...] = jnp.dot(picks[1], spectra[1 + e, rows(0, h)], preferred_element_type=jnp.float32)
            for c in range(COMP):
                at = pl.ds(c * 2 * SLOTS, 2 * SLOTS)
                lr, li, lm = left[h, at, 0:256], left[h, at, 256:512], left[h, at, 512:640]
                rr, ri, rm = right[at, 0:256], right[at, 256:512], right[at, 512:640]
                total[:, 0:256] += lr * rr + li * ri
                total[:, 256:512] += lr * ri - li * rr
                total[:, 512:640] += lm * rm
                total[:, 640:768] += lm * pltpu.roll(rm, 64, 1)

        real, imag, both, cross = total[:, 0:256], total[:, 256:512], total[:, 512:640], total[:, 640:768]
        imag = jnp.where(theirs_row, -imag, imag)
        cross = jnp.where(theirs_row[:, :128], -cross, cross)
        curves = jnp.dot(
            jnp.concatenate([real, imag, both, cross], axis=1).astype(jnp.bfloat16),
            inverse[...],
            preferred_element_type=jnp.float32,
        )
        for k in range(2 * GROUP):
            piece = curves[8 * k : 8 * k + 8]
            shares[e, k] = jnp.concatenate([piece[:, :128], piece[:, 128:]], axis=0).astype(jnp.bfloat16)
        for side in range(2):
            for d in range(GROUP):
                if e == 2 or side == 1 or d > 0:
                    share(e, side, d).start()
        if e < 2:
            gathered[e, pl.ds(group, 1)] = shares[e, pl.ds(group, 1)]

    pl.semaphore_wait(settled, GROUP - 1)
    work(1)

    @pl.when(late == 0)
    def _():
        work(0)

    work(2)

    @pl.when(late == 1)
    def _():
        work(0)

    slot = group * 8 + lax.rem(lax.broadcasted_iota(jnp.int32, (16, 128), 0), 8)
    for e in range(ROUNDS):
        for side in range(2):
            for d in range(GROUP):
                if e == 2 or side == 1 or d > 0:
                    landed(e, side, d).wait_recv()
        curve = jnp.sum(gathered[e].astype(jnp.float32), axis=0)
        curve = jnp.where(slot < counts_ref[0, e], curve, 0.0)
        out_ref[e, :, 0:128] = curve[0:8]
        out_ref[e, :, 128:256] = curve[8:16]

    for e in range(ROUNDS):
        listing(e).wait_send()
        for h in range(HALVES):
            wave(e, h).wait_send()
        if e == 1:

            @pl.when(late == 0)
            def _():
                wave(1, 2).wait_send()

        if e == 2:

            @pl.when(late == 1)
            def _():
                wave(2, 2).wait_send()
                wave(2, 3).wait_send()

        for side in range(2):
            for d in range(GROUP):
                if e == 2 or side == 1 or d > 0:
                    share(e, side, d).wait_send()


def shards(waveforms, pair_lists, pair_counts):
    forward, inverse = tables()
    bf16, f32 = jnp.bfloat16, jnp.float32
    dma = pltpu.SemaphoreType.DMA
    return pl.pallas_call(
        kernel,
        out_shape=jax.ShapeDtypeStruct((ROUNDS, 8, LAGS), f32),
        in_specs=[
            pl.BlockSpec(memory_space=pl.ANY),
            pl.BlockSpec(memory_space=pl.ANY),
            pl.BlockSpec(memory_space=pl.ANY),
            pl.BlockSpec(memory_space=pl.ANY),
            pl.BlockSpec(memory_space=pl.ANY),
        ],
        out_specs=pl.BlockSpec(memory_space=pltpu.VMEM),
        scratch_shapes=[
            pltpu.VMEM((EVENTS, COMP, GROUP, LENGTH), bf16),
            pltpu.VMEM((ROUNDS, 2, SLOTS), jnp.int32),
            pltpu.SMEM((1, ROUNDS), jnp.int32),
            pltpu.VMEM((LENGTH, PERIOD), bf16),
            pltpu.VMEM((WIDE, LAGS), bf16),
            pltpu.VMEM((TRACES, LENGTH), bf16),
            pltpu.VMEM((ROUNDS, (HALVES + 1) * CHUNK, LENGTH), bf16),
            pltpu.VMEM((1 + ROUNDS, (HALVES + 1) * CHUNK, PERIOD), bf16),
            pltpu.VMEM((HALVES + 1, COMP * 2 * SLOTS, PERIOD), f32),
            pltpu.VMEM((COMP * 2 * SLOTS, PERIOD), f32),
            pltpu.VMEM((2 * SLOTS, WIDE), f32),
            pltpu.VMEM((8, 128), jnp.int32),
            pltpu.VMEM((ROUNDS, 8, 128), jnp.int32),
            pltpu.VMEM((2, COMP * 2 * SLOTS, CHUNK), bf16),
            pltpu.VMEM((ROUNDS, 2 * GROUP, 16, 128), bf16),
            pltpu.VMEM((ROUNDS, 2 * GROUP, 16, 128), bf16),
            dma((5,)),
            dma((ROUNDS, 2 * HALVES)),
            dma((ROUNDS, 2 * HALVES)),
            dma((ROUNDS,)),
            dma((ROUNDS,)),
            dma((ROUNDS, 2 * GROUP)),
            dma((ROUNDS, 2 * GROUP)),
            pltpu.SemaphoreType.REGULAR,
            pltpu.SemaphoreType.REGULAR,
        ],
        compiler_params=pltpu.CompilerParams(
            collective_id=0, has_side_effects=True, vmem_limit_bytes=GRANT
        ),
        name="correlate",
    )(
        jnp.transpose(waveforms, (0, 2, 1, 3)),
        jnp.transpose(pair_lists, (0, 2, 1)),
        jnp.transpose(pair_counts, (1, 0)),
        jnp.asarray(forward),
        jnp.asarray(inverse),
    )


def solution(mesh):
    return jax.shard_map(
        shards,
        mesh=mesh,
        in_specs=(P("region", "station", None, None), P(None, "region", None), P(None, "region")),
        out_specs=P(None, ("region", "station"), None),
        check_vma=False,
    )
```

```python
import math

import jax
import jax.numpy as jnp
import numpy as np
from jax import lax
from jax.experimental import pallas as pl
from jax.experimental.pallas import tpu as pltpu
from jax.sharding import PartitionSpec as P

MESH = pl.DeviceIdType.MESH
ROUNDS = 3
EVENTS = 16
GROUP = 4
COMP = 3
LENGTH = 512
LAGS = 256
SLOTS = 32
STATIONS = 16
EPS = 1e-06
CHUNK = COMP * EVENTS
TRACES = GROUP * CHUNK
PERIOD = LENGTH + LAGS // 2
HALF = PERIOD // 2
WIDE = 3 * LAGS
GRANT = 55200 * 2**10
HALVES = 2
SHIFT = 2
LEFT_OUT = SHIFT * EVENTS


def tables():
    order = np.arange(HALF)
    times = np.arange(LENGTH)[:, None]
    angle = 2.0 * np.pi * ((2 * order[None, :] + 1) * times % (2 * PERIOD)) / (2 * PERIOD)
    real, imag = np.cos(angle), -np.sin(angle)
    forward = np.concatenate([real[:, :256], imag[:, :256], real[:, 256:], imag[:, 256:]], axis=1)
    lags = np.arange(LAGS)[None, :] - LAGS // 2
    angle = 2.0 * np.pi * ((2 * order[:, None] + 1) * lags % (2 * PERIOD)) / (2 * PERIOD)
    factor = 2.0 / (PERIOD * math.sqrt(STATIONS * COMP * LENGTH))
    cos, sin = factor * np.cos(angle), factor * np.sin(angle)
    inverse = np.concatenate(
        [cos[:256], -sin[:256], cos[256:], cos[256:], -sin[256:], sin[256:]], axis=0
    )
    return forward.astype(jnp.bfloat16), inverse.astype(jnp.bfloat16)


def kernel(
    x_hbm, lists_hbm, counts_hbm, forward_hbm, inverse_hbm, out_ref,
    x_in, lists_ref, counts_ref, forward, inverse, normal, arrived, spectra, left, right, total,
    message, heard, picks, shares, gathered,
    load_sem, wave_out, wave_in, list_out, list_in, share_out, share_in, ready, settled,
):
    region, group = lax.axis_index("region"), lax.axis_index("station")
    z = lax.rem(region, 8)
    bits = [lax.rem(z // (1 << e), 2) for e in range(ROUNDS)]
    step = [(1 << e) * (1 - 2 * bits[e]) for e in range(ROUNDS)]
    partner = [region + step[0], region + step[1], region + step[1] + step[2]]
    mates = [lax.rem(group + d, GROUP) for d in range(GROUP)]
    late = bits[2]
    odd = lax.rem(bits[0] + bits[1] + bits[2], 2)
    worked, sent = odd * HALVES * CHUNK, (1 - odd) * HALVES * CHUNK

    arrived[1, HALVES * CHUNK :] = jnp.zeros_like(arrived[1, HALVES * CHUNK :])
    arrived[2, HALVES * CHUNK - LEFT_OUT :] = jnp.zeros_like(arrived[2, HALVES * CHUNK - LEFT_OUT :])
    barrier = pltpu.get_barrier_semaphore()

    def greet(which, to):
        pl.semaphore_signal(which, inc=1, device_id=to, device_id_type=MESH)

    greet(barrier, (partner[1], group))
    greet(barrier, (partner[0], group))
    for d in range(1, GROUP):
        greet(barrier, (region, mates[d]))

    @pl.when(late == 0)
    def _():
        greet(barrier, (partner[2], group))

    loads = [
        pltpu.make_async_copy(x_hbm, x_in, load_sem.at[0]),
        pltpu.make_async_copy(forward_hbm, forward, load_sem.at[1]),
        pltpu.make_async_copy(inverse_hbm, inverse, load_sem.at[2]),
        pltpu.make_async_copy(lists_hbm, lists_ref, load_sem.at[3]),
        pltpu.make_async_copy(counts_hbm, counts_ref, load_sem.at[4]),
    ]
    for load in loads:
        load.start()

    loads[3].wait()
    message[...] = jnp.zeros_like(message)
    for e in range(ROUNDS):
        message[2 * e : 2 * e + 2, 0:SLOTS] = lists_ref[e]
    mine = message[...]
    turned = pltpu.roll(mine, SLOTS, 1)
    even = lax.rem(lax.broadcasted_iota(jnp.int32, (8, 128), 0), 2) == 0
    turned = jnp.where(even, pltpu.roll(turned, 7, 0), pltpu.roll(turned, 1, 0))
    message[...] = mine + turned

    row = lax.broadcasted_iota(jnp.int32, (TRACES, TRACES), 0)
    column = lax.broadcasted_iota(jnp.int32, (TRACES, TRACES), 1)
    source = lax.rem(row, EVENTS) * (COMP * GROUP) + lax.rem(row // EVENTS, COMP) * GROUP + row // CHUNK
    reorder = jnp.where(column == source, 1.0, 0.0).astype(jnp.bfloat16)
    loads[0].wait()
    traces = x_in[...].astype(jnp.float32).reshape(TRACES, LENGTH)
    traces = traces - jnp.mean(traces, axis=-1, keepdims=True)
    traces = traces * lax.rsqrt(jnp.mean(traces * traces, axis=-1, keepdims=True) + EPS)
    normal[...] = jnp.dot(
        reorder, traces.astype(jnp.bfloat16), preferred_element_type=jnp.float32
    ).astype(jnp.bfloat16)

    def rows(base, h):
        return pl.ds(pl.multiple_of(base + h * CHUNK, CHUNK), CHUNK)

    def copy(e, h, src, dst, size):
        return pltpu.make_async_remote_copy(
            src_ref=normal.at[pl.ds(pl.multiple_of(src, EVENTS), size)],
            dst_ref=arrived.at[e, pl.ds(dst, size)],
            send_sem=wave_out.at[e, h],
            recv_sem=wave_in.at[e, h],
            device_id=(partner[e], group),
            device_id_type=MESH,
        )

    last = HALVES * CHUNK - LEFT_OUT

    def wave(e, h):
        if e < 2:
            if h < HALVES:
                return copy(e, h, sent + h * CHUNK, h * CHUNK, CHUNK)
            return copy(e, h, worked + last, last + CHUNK, LEFT_OUT)
        if h == 0:
            return copy(e, h, worked, 0, CHUNK)
        if h == 1:
            return copy(e, h, worked + CHUNK, CHUNK, CHUNK - LEFT_OUT)
        if h == 2:
            return copy(e, h, worked + last, last, LEFT_OUT)
        return copy(e, h, sent + last, last + CHUNK, LEFT_OUT)

    def listing(e):
        return pltpu.make_async_remote_copy(
            src_ref=message,
            dst_ref=heard.at[e],
            send_sem=list_out.at[e],
            recv_sem=list_in.at[e],
            device_id=(partner[e], group),
            device_id_type=MESH,
        )

    def share(e, side, d):
        to = partner[e] if side == 1 else partner[1] if e == 2 else region
        return pltpu.make_async_remote_copy(
            src_ref=shares.at[e, GROUP * side + mates[d]],
            dst_ref=gathered.at[e, GROUP * side + group],
            send_sem=share_out.at[e],
            recv_sem=share_in.at[e],
            device_id=(to, mates[d]),
            device_id_type=MESH,
        )

    def all_shares(e):
        size = 2 * GROUP if e == 2 else 2 * GROUP - 1
        return pltpu.make_async_remote_copy(
            src_ref=shares.at[e, pl.ds(0, size)],
            dst_ref=gathered.at[e, pl.ds(0, size)],
            send_sem=share_out.at[e],
            recv_sem=share_in.at[e],
            device_id=(partner[e], group),
            device_id_type=MESH,
        )

    def send(e):
        listing(e).start()
        for h in range(HALVES):
            wave(e, h).start()

    @pl.when(late == 0)
    def _():
        pl.semaphore_wait(barrier, 5)

    @pl.when(late == 1)
    def _():
        pl.semaphore_wait(barrier, 6)
        greet(ready, (partner[2], group))
        send(2)
        wave(2, 2).start()
        wave(2, 3).start()

    send(1)
    send(0)

    @pl.when(late == 0)
    def _():
        wave(1, 2).start()

    loads[1].wait()
    spectra[0, : HALVES * CHUNK] = jnp.dot(
        normal[pl.ds(pl.multiple_of(worked, CHUNK), HALVES * CHUNK)], forward[...], preferred_element_type=jnp.float32
    ).astype(jnp.bfloat16)
    loads[2].wait()
    loads[4].wait()

    @pl.when(late == 0)
    def _():
        pl.semaphore_wait(ready, 1)
        send(2)

    for d in range(1, GROUP):
        greet(settled, (region, mates[d]))

    lane = lax.broadcasted_iota(jnp.int32, (8, 128), 1)
    cell = lax.broadcasted_iota(jnp.int32, (COMP * 2 * SLOTS, CHUNK), 1)
    part = lax.broadcasted_iota(jnp.int32, (COMP * 2 * SLOTS, CHUNK), 0) // (2 * SLOTS) * EVENTS
    theirs_row = lax.broadcasted_iota(jnp.int32, (2 * SLOTS, LAGS), 0) >= SLOTS

    def work(e):
        listing(e).wait_recv()
        events = jnp.where(lane < SLOTS, heard[1] if e == 2 else message[...], heard[e]).astype(jnp.float32).T
        for side in range(2):
            event = events[: 2 * SLOTS, 2 * e + side : 2 * e + side + 1].astype(jnp.int32)
            event = jnp.concatenate([event] * COMP, axis=0)
            picks[side] = jnp.where(cell == part + event, 1.0, 0.0).astype(jnp.bfloat16)
        total[...] = jnp.zeros_like(total)
        known = 2 if e == 2 else 0

        def pick_left(h):
            left[h] = jnp.dot(picks[0], spectra[known, h * CHUNK : (h + 1) * CHUNK], preferred_element_type=jnp.float32)

        for h in range(HALVES):
            pick_left(h)
        if e == 2:

            @pl.when(late == 0)
            def _():
                wave(1, 2).wait_recv()
                spectra[2, HALVES * CHUNK :] = jnp.dot(
                    arrived[1, HALVES * CHUNK :], forward[...], preferred_element_type=jnp.float32
                ).astype(jnp.bfloat16)
                pick_left(2)

        @pl.loop(0, HALVES + 1 - late if e == 2 else HALVES)
        def _(h):
            for k in range(HALVES):

                @pl.when(h == k)
                def _(k=k):
                    wave(e, k).wait_recv()

            if e == 2:
                for k in range(HALVES):

                    @pl.when((late == 0) & (h == k + 1))
                    def _(k=k):
                        wave(2, k + 2).wait_recv()

            spectra[1 + e, rows(0, h)] = jnp.dot(
                arrived[e, rows(0, h)], forward[...], preferred_element_type=jnp.float32
            ).astype(jnp.bfloat16)
            right[...] = jnp.dot(picks[1], spectra[1 + e, rows(0, h)], preferred_element_type=jnp.float32)
            for g in range(2 * SLOTS // 16):
                to = pl.ds(16 * g, 16)
                sums = [total[to, 0:256], total[to, 256:512], total[to, 512:640], total[to, 640:768]]
                for c in range(COMP):
                    at = pl.ds(c * 2 * SLOTS + 16 * g, 16)
                    lr, li, lm = left[h, at, 0:256], left[h, at, 256:512], left[h, at, 512:640]
                    rr, ri, rm = right[at, 0:256], right[at, 256:512], right[at, 512:640]
                    sums[0] += lr * rr + li * ri
                    sums[1] += lr * ri - li * rr
                    sums[2] += lm * rm
                    sums[3] += lm * pltpu.roll(rm, 64, 1)
                total[to, 0:256], total[to, 256:512], total[to, 512:640], total[to, 640:768] = sums

        real, imag, both, cross = total[:, 0:256], total[:, 256:512], total[:, 512:640], total[:, 640:768]
        imag = jnp.where(theirs_row, -imag, imag)
        cross = jnp.where(theirs_row[:, :128], -cross, cross)
        curves = jnp.dot(
            jnp.concatenate([real, imag, both, cross], axis=1).astype(jnp.bfloat16),
            inverse[...],
            preferred_element_type=jnp.float32,
        )
        for k in range(2 * GROUP):
            piece = curves[8 * k : 8 * k + 8]
            shares[e, k] = jnp.concatenate([piece[:, :128], piece[:, 128:]], axis=0).astype(jnp.bfloat16)
        for side in range(2):
            for d in range(GROUP):
                if e == 2 or side == 1 or d > 0:
                    share(e, side, d).start()
        if e < 2:
            gathered[e, pl.ds(group, 1)] = shares[e, pl.ds(group, 1)]

    pl.semaphore_wait(settled, GROUP - 1)
    work(1)

    @pl.when(late == 0)
    def _():
        work(0)

    work(2)

    @pl.when(late == 1)
    def _():
        work(0)

    for e in range(ROUNDS):
        listing(e).wait_send()
        for h in range(HALVES):
            wave(e, h).wait_send()

    @pl.when(late == 0)
    def _():
        wave(1, 2).wait_send()

    @pl.when(late == 1)
    def _():
        wave(2, 2).wait_send()
        wave(2, 3).wait_send()


    slot = group * 8 + lax.rem(lax.broadcasted_iota(jnp.int32, (16, 128), 0), 8)
    for e in range(ROUNDS):
        all_shares(e).wait_recv()
        curve = jnp.sum(gathered[e].astype(jnp.float32), axis=0)
        curve = jnp.where(slot < counts_ref[0, e], curve, 0.0)
        out_ref[e, :, 0:128] = curve[0:8]
        out_ref[e, :, 128:256] = curve[8:16]

    for e in range(ROUNDS):
        all_shares(e).wait_send()


def shards(waveforms, pair_lists, pair_counts):
    forward, inverse = tables()
    bf16, f32 = jnp.bfloat16, jnp.float32
    dma = pltpu.SemaphoreType.DMA
    return pl.pallas_call(
        kernel,
        out_shape=jax.ShapeDtypeStruct((ROUNDS, 8, LAGS), f32),
        in_specs=[
            pl.BlockSpec(memory_space=pl.ANY),
            pl.BlockSpec(memory_space=pl.ANY),
            pl.BlockSpec(memory_space=pl.ANY),
            pl.BlockSpec(memory_space=pl.ANY),
            pl.BlockSpec(memory_space=pl.ANY),
        ],
        out_specs=pl.BlockSpec(memory_space=pltpu.VMEM),
        scratch_shapes=[
            pltpu.VMEM((EVENTS, COMP, GROUP, LENGTH), bf16),
            pltpu.VMEM((ROUNDS, 2, SLOTS), jnp.int32),
            pltpu.SMEM((1, ROUNDS), jnp.int32),
            pltpu.VMEM((LENGTH, PERIOD), bf16),
            pltpu.VMEM((WIDE, LAGS), bf16),
            pltpu.VMEM((TRACES, LENGTH), bf16),
            pltpu.VMEM((ROUNDS, (HALVES + 1) * CHUNK, LENGTH), bf16),
            pltpu.VMEM((1 + ROUNDS, (HALVES + 1) * CHUNK, PERIOD), bf16),
            pltpu.VMEM((HALVES + 1, COMP * 2 * SLOTS, PERIOD), f32),
            pltpu.VMEM((COMP * 2 * SLOTS, PERIOD), f32),
            pltpu.VMEM((2 * SLOTS, WIDE), f32),
            pltpu.VMEM((8, 128), jnp.int32),
            pltpu.VMEM((ROUNDS, 8, 128), jnp.int32),
            pltpu.VMEM((2, COMP * 2 * SLOTS, CHUNK), bf16),
            pltpu.VMEM((ROUNDS, 2 * GROUP, 16, 128), bf16),
            pltpu.VMEM((ROUNDS, 2 * GROUP, 16, 128), bf16),
            dma((5,)),
            dma((ROUNDS, 2 * HALVES)),
            dma((ROUNDS, 2 * HALVES)),
            dma((ROUNDS,)),
            dma((ROUNDS,)),
            dma((ROUNDS,)),
            dma((ROUNDS,)),
            pltpu.SemaphoreType.REGULAR,
            pltpu.SemaphoreType.REGULAR,
        ],
        compiler_params=pltpu.CompilerParams(
            collective_id=0, has_side_effects=True, vmem_limit_bytes=GRANT
        ),
        name="correlate",
    )(
        jnp.transpose(waveforms, (0, 2, 1, 3)),
        pltpu.with_memory_space_constraint(jnp.transpose(pair_lists, (0, 2, 1)), pltpu.HBM),
        pltpu.with_memory_space_constraint(jnp.transpose(pair_counts, (1, 0)), pltpu.HBM),
        jnp.asarray(forward),
        jnp.asarray(inverse),
    )


def solution(mesh):
    return jax.shard_map(
        shards,
        mesh=mesh,
        in_specs=(P("region", "station", None, None), P(None, "region", None), P(None, "region")),
        out_specs=P(None, ("region", "station"), None),
        check_vma=False,
    )
```

```python
import math

import jax
import jax.numpy as jnp
import numpy as np
from jax import lax
from jax.experimental import pallas as pl
from jax.experimental.pallas import tpu as pltpu
from jax.sharding import PartitionSpec as P

MESH = pl.DeviceIdType.MESH
ROUNDS = 3
EVENTS = 16
GROUP = 4
COMP = 3
LENGTH = 512
LAGS = 256
SLOTS = 32
STATIONS = 16
EPS = 1e-06
CHUNK = COMP * EVENTS
TRACES = GROUP * CHUNK
PERIOD = LENGTH + LAGS // 2
HALF = PERIOD // 2
WIDE = 3 * LAGS
GRANT = 55200 * 2**10
HALVES = 2
SHIFT = 2
LEFT_OUT = SHIFT * EVENTS


def tables():
    order = np.arange(HALF)
    times = np.arange(LENGTH)[:, None]
    angle = 2.0 * np.pi * ((2 * order[None, :] + 1) * times % (2 * PERIOD)) / (2 * PERIOD)
    real, imag = np.cos(angle), -np.sin(angle)
    forward = np.concatenate([real[:, :256], imag[:, :256], real[:, 256:], imag[:, 256:]], axis=1)
    lags = np.arange(LAGS)[None, :] - LAGS // 2
    angle = 2.0 * np.pi * ((2 * order[:, None] + 1) * lags % (2 * PERIOD)) / (2 * PERIOD)
    factor = 2.0 / (PERIOD * math.sqrt(STATIONS * COMP * LENGTH))
    cos, sin = factor * np.cos(angle), factor * np.sin(angle)
    inverse = np.concatenate(
        [cos[:256], -sin[:256], cos[256:], cos[256:], -sin[256:], sin[256:]], axis=0
    )
    return forward.astype(jnp.bfloat16), inverse.astype(jnp.bfloat16)


def kernel(
    x_hbm, lists_hbm, counts_hbm, forward_hbm, inverse_hbm, out_ref,
    x_in, lists_ref, counts_ref, forward, inverse, normal, arrived, spectra, left, right, total,
    message, heard, picks, shares, gathered,
    load_sem, wave_out, wave_in, list_out, list_in, share_out, share_in, ready, settled,
):
    region, group = lax.axis_index("region"), lax.axis_index("station")
    z = lax.rem(region, 8)
    bits = [lax.rem(z // (1 << e), 2) for e in range(ROUNDS)]
    step = [(1 << e) * (1 - 2 * bits[e]) for e in range(ROUNDS)]
    partner = [region + step[0], region + step[1], region + step[1] + step[2]]
    mates = [lax.rem(group + d, GROUP) for d in range(GROUP)]
    late = bits[2]
    odd = lax.rem(bits[0] + bits[1] + bits[2], 2)
    worked, sent = odd * HALVES * CHUNK, (1 - odd) * HALVES * CHUNK

    arrived[1, HALVES * CHUNK :] = jnp.zeros_like(arrived[1, HALVES * CHUNK :])
    arrived[2, HALVES * CHUNK - LEFT_OUT :] = jnp.zeros_like(arrived[2, HALVES * CHUNK - LEFT_OUT :])
    barrier = pltpu.get_barrier_semaphore()

    def greet(which, to):
        pl.semaphore_signal(which, inc=1, device_id=to, device_id_type=MESH)

    greet(barrier, (partner[1], group))
    greet(barrier, (partner[0], group))
    for d in range(1, GROUP):
        greet(barrier, (region, mates[d]))

    @pl.when(late == 0)
    def _():
        greet(barrier, (partner[2], group))

    loads = [
        pltpu.make_async_copy(x_hbm, x_in, load_sem.at[0]),
        pltpu.make_async_copy(forward_hbm, forward, load_sem.at[1]),
        pltpu.make_async_copy(inverse_hbm, inverse, load_sem.at[2]),
        pltpu.make_async_copy(lists_hbm, lists_ref, load_sem.at[3]),
        pltpu.make_async_copy(counts_hbm, counts_ref, load_sem.at[4]),
    ]
    for k in (3, 0, 1, 2, 4):
        loads[k].start()

    loads[3].wait()
    message[...] = jnp.zeros_like(message)
    for e in range(ROUNDS):
        message[2 * e : 2 * e + 2, 0:SLOTS] = lists_ref[e]
    mine = message[...]
    turned = pltpu.roll(mine, SLOTS, 1)
    even = lax.rem(lax.broadcasted_iota(jnp.int32, (8, 128), 0), 2) == 0
    turned = jnp.where(even, pltpu.roll(turned, 7, 0), pltpu.roll(turned, 1, 0))
    message[...] = mine + turned

    row = lax.broadcasted_iota(jnp.int32, (TRACES, TRACES), 0)
    column = lax.broadcasted_iota(jnp.int32, (TRACES, TRACES), 1)
    source = lax.rem(row, EVENTS) * (COMP * GROUP) + lax.rem(row // EVENTS, COMP) * GROUP + row // CHUNK
    reorder = jnp.where(column == source, 1.0, 0.0).astype(jnp.bfloat16)
    loads[0].wait()
    traces = x_in[...].astype(jnp.float32).reshape(TRACES, LENGTH)
    traces = traces - jnp.mean(traces, axis=-1, keepdims=True)
    traces = traces * lax.rsqrt(jnp.mean(traces * traces, axis=-1, keepdims=True) + EPS)
    normal[...] = jnp.dot(
        reorder, traces.astype(jnp.bfloat16), preferred_element_type=jnp.float32
    ).astype(jnp.bfloat16)

    def rows(base, h):
        return pl.ds(pl.multiple_of(base + h * CHUNK, CHUNK), CHUNK)

    def copy(e, h, src, dst, size):
        return pltpu.make_async_remote_copy(
            src_ref=normal.at[pl.ds(pl.multiple_of(src, EVENTS), size)],
            dst_ref=arrived.at[e, pl.ds(dst, size)],
            send_sem=wave_out.at[e, h],
            recv_sem=wave_in.at[e, h],
            device_id=(partner[e], group),
            device_id_type=MESH,
        )

    last = HALVES * CHUNK - LEFT_OUT

    def wave(e, h):
        if e < 2:
            if h < HALVES:
                return copy(e, h, sent + h * CHUNK, h * CHUNK, CHUNK)
            return copy(e, h, worked + last, last + CHUNK, LEFT_OUT)
        if h == 0:
            return copy(e, h, worked, 0, CHUNK)
        if h == 1:
            return copy(e, h, worked + CHUNK, CHUNK, CHUNK - LEFT_OUT)
        if h == 2:
            return copy(e, h, worked + last, last, LEFT_OUT)
        return copy(e, h, sent + last, last + CHUNK, LEFT_OUT)

    def listing(e):
        return pltpu.make_async_remote_copy(
            src_ref=message,
            dst_ref=heard.at[e],
            send_sem=list_out.at[e],
            recv_sem=list_in.at[e],
            device_id=(partner[e], group),
            device_id_type=MESH,
        )

    def share(e, side, d):
        to = partner[e] if side == 1 else partner[1] if e == 2 else region
        return pltpu.make_async_remote_copy(
            src_ref=shares.at[e, GROUP * side + mates[d]],
            dst_ref=gathered.at[e, GROUP * side + group],
            send_sem=share_out.at[e],
            recv_sem=share_in.at[e],
            device_id=(to, mates[d]),
            device_id_type=MESH,
        )

    def all_shares(e):
        size = 2 * GROUP if e == 2 else 2 * GROUP - 1
        return pltpu.make_async_remote_copy(
            src_ref=shares.at[e, pl.ds(0, size)],
            dst_ref=gathered.at[e, pl.ds(0, size)],
            send_sem=share_out.at[e],
            recv_sem=share_in.at[e],
            device_id=(partner[e], group),
            device_id_type=MESH,
        )

    def send(e):
        listing(e).start()
        for h in range(HALVES):
            wave(e, h).start()

    @pl.when(late == 0)
    def _():
        pl.semaphore_wait(barrier, 5)

    @pl.when(late == 1)
    def _():
        pl.semaphore_wait(barrier, 6)
        greet(ready, (partner[2], group))
        send(2)
        wave(2, 2).start()
        wave(2, 3).start()

    send(1)
    send(0)

    @pl.when(late == 0)
    def _():
        wave(1, 2).start()

    loads[1].wait()
    spectra[0, : HALVES * CHUNK] = jnp.dot(
        normal[pl.ds(pl.multiple_of(worked, CHUNK), HALVES * CHUNK)], forward[...], preferred_element_type=jnp.float32
    ).astype(jnp.bfloat16)
    loads[2].wait()
    loads[4].wait()

    @pl.when(late == 0)
    def _():
        pl.semaphore_wait(ready, 1)
        send(2)

    for d in range(1, GROUP):
        greet(settled, (region, mates[d]))

    lane = lax.broadcasted_iota(jnp.int32, (8, 128), 1)
    cell = lax.broadcasted_iota(jnp.int32, (COMP * 2 * SLOTS, CHUNK), 1)
    part = lax.broadcasted_iota(jnp.int32, (COMP * 2 * SLOTS, CHUNK), 0) // (2 * SLOTS) * EVENTS
    theirs_row = lax.broadcasted_iota(jnp.int32, (2 * SLOTS, LAGS), 0) >= SLOTS

    def work(e):
        listing(e).wait_recv()
        events = jnp.where(lane < SLOTS, heard[1] if e == 2 else message[...], heard[e]).astype(jnp.float32).T
        for side in range(2):
            event = events[: 2 * SLOTS, 2 * e + side : 2 * e + side + 1].astype(jnp.int32)
            event = jnp.concatenate([event] * COMP, axis=0)
            picks[side] = jnp.where(cell == part + event, 1.0, 0.0).astype(jnp.bfloat16)
        total[...] = jnp.zeros_like(total)
        known = 2 if e == 2 else 0

        def pick_left(h):
            left[h] = jnp.dot(picks[0], spectra[known, h * CHUNK : (h + 1) * CHUNK], preferred_element_type=jnp.float32)

        for h in range(HALVES):
            pick_left(h)
        if e == 2:

            @pl.when(late == 0)
            def _():
                wave(1, 2).wait_recv()
                spectra[2, HALVES * CHUNK :] = jnp.dot(
                    arrived[1, HALVES * CHUNK :], forward[...], preferred_element_type=jnp.float32
                ).astype(jnp.bfloat16)
                pick_left(2)

        def unit(h):
            spectra[1 + e, h * CHUNK : (h + 1) * CHUNK] = jnp.dot(
                arrived[e, h * CHUNK : (h + 1) * CHUNK], forward[...], preferred_element_type=jnp.float32
            ).astype(jnp.bfloat16)
            right[...] = jnp.dot(picks[1], spectra[1 + e, h * CHUNK : (h + 1) * CHUNK], preferred_element_type=jnp.float32)
            for g in range(2 * SLOTS // 16):
                to = pl.ds(16 * g, 16)
                sums = [total[to, 0:256], total[to, 256:512], total[to, 512:640], total[to, 640:768]]
                for c in range(COMP):
                    at = pl.ds(c * 2 * SLOTS + 16 * g, 16)
                    lr, li, lm = left[h, at, 0:256], left[h, at, 256:512], left[h, at, 512:640]
                    rr, ri, rm = right[at, 0:256], right[at, 256:512], right[at, 512:640]
                    sums[0] += lr * rr + li * ri
                    sums[1] += lr * ri - li * rr
                    sums[2] += lm * rm
                    sums[3] += lm * pltpu.roll(rm, 64, 1)
                total[to, 0:256], total[to, 256:512], total[to, 512:640], total[to, 640:768] = sums

        for h in range(HALVES):
            wave(e, h).wait_recv()
            if e == 2 and h == 1:

                @pl.when(late == 0)
                def _():
                    wave(2, 2).wait_recv()

            unit(h)
        if e == 2:

            @pl.when(late == 0)
            def _():
                wave(2, 3).wait_recv()
                unit(2)

        real, imag, both, cross = total[:, 0:256], total[:, 256:512], total[:, 512:640], total[:, 640:768]
        imag = jnp.where(theirs_row, -imag, imag)
        cross = jnp.where(theirs_row[:, :128], -cross, cross)
        curves = jnp.dot(
            jnp.concatenate([real, imag, both, cross], axis=1).astype(jnp.bfloat16),
            inverse[...],
            preferred_element_type=jnp.float32,
        )
        for k in range(2 * GROUP):
            piece = curves[8 * k : 8 * k + 8]
            shares[e, k] = jnp.concatenate([piece[:, :128], piece[:, 128:]], axis=0).astype(jnp.bfloat16)
        for side in range(2):
            for d in range(GROUP):
                if e == 2 or side == 1 or d > 0:
                    share(e, side, d).start()
        if e < 2:
            gathered[e, pl.ds(group, 1)] = shares[e, pl.ds(group, 1)]

    pl.semaphore_wait(settled, GROUP - 1)
    work(1)

    @pl.when(late == 0)
    def _():
        work(0)

    work(2)

    @pl.when(late == 1)
    def _():
        work(0)

    for e in range(ROUNDS):
        listing(e).wait_send()
        for h in range(HALVES):
            wave(e, h).wait_send()

    @pl.when(late == 0)
    def _():
        wave(1, 2).wait_send()

    @pl.when(late == 1)
    def _():
        wave(2, 2).wait_send()
        wave(2, 3).wait_send()


    slot = group * 8 + lax.rem(lax.broadcasted_iota(jnp.int32, (16, 128), 0), 8)
    for e in range(ROUNDS):
        all_shares(e).wait_recv()
        curve = jnp.sum(gathered[e].astype(jnp.float32), axis=0)
        curve = jnp.where(slot < counts_ref[0, e], curve, 0.0)
        out_ref[e, :, 0:128] = curve[0:8]
        out_ref[e, :, 128:256] = curve[8:16]

    for e in range(ROUNDS):
        all_shares(e).wait_send()


def shards(waveforms, pair_lists, pair_counts):
    forward, inverse = tables()
    bf16, f32 = jnp.bfloat16, jnp.float32
    dma = pltpu.SemaphoreType.DMA
    return pl.pallas_call(
        kernel,
        out_shape=jax.ShapeDtypeStruct((ROUNDS, 8, LAGS), f32),
        in_specs=[
            pl.BlockSpec(memory_space=pl.ANY),
            pl.BlockSpec(memory_space=pl.ANY),
            pl.BlockSpec(memory_space=pl.ANY),
            pl.BlockSpec(memory_space=pl.ANY),
            pl.BlockSpec(memory_space=pl.ANY),
        ],
        out_specs=pl.BlockSpec(memory_space=pltpu.VMEM),
        scratch_shapes=[
            pltpu.VMEM((EVENTS, COMP, GROUP, LENGTH), bf16),
            pltpu.VMEM((ROUNDS, 2, SLOTS), jnp.int32),
            pltpu.SMEM((1, ROUNDS), jnp.int32),
            pltpu.VMEM((LENGTH, PERIOD), bf16),
            pltpu.VMEM((WIDE, LAGS), bf16),
            pltpu.VMEM((TRACES, LENGTH), bf16),
            pltpu.VMEM((ROUNDS, (HALVES + 1) * CHUNK, LENGTH), bf16),
            pltpu.VMEM((1 + ROUNDS, (HALVES + 1) * CHUNK, PERIOD), bf16),
            pltpu.VMEM((HALVES + 1, COMP * 2 * SLOTS, PERIOD), f32),
            pltpu.VMEM((COMP * 2 * SLOTS, PERIOD), f32),
            pltpu.VMEM((2 * SLOTS, WIDE), f32),
            pltpu.VMEM((8, 128), jnp.int32),
            pltpu.VMEM((ROUNDS, 8, 128), jnp.int32),
            pltpu.VMEM((2, COMP * 2 * SLOTS, CHUNK), bf16),
            pltpu.VMEM((ROUNDS, 2 * GROUP, 16, 128), bf16),
            pltpu.VMEM((ROUNDS, 2 * GROUP, 16, 128), bf16),
            dma((5,)),
            dma((ROUNDS, 2 * HALVES)),
            dma((ROUNDS, 2 * HALVES)),
            dma((ROUNDS,)),
            dma((ROUNDS,)),
            dma((ROUNDS,)),
            dma((ROUNDS,)),
            pltpu.SemaphoreType.REGULAR,
            pltpu.SemaphoreType.REGULAR,
        ],
        compiler_params=pltpu.CompilerParams(
            collective_id=0, has_side_effects=True, vmem_limit_bytes=GRANT
        ),
        name="correlate",
    )(
        jnp.transpose(waveforms, (0, 2, 1, 3)),
        pltpu.with_memory_space_constraint(jnp.transpose(pair_lists, (0, 2, 1)), pltpu.HBM),
        pltpu.with_memory_space_constraint(jnp.transpose(pair_counts, (1, 0)), pltpu.HBM),
        jnp.asarray(forward),
        jnp.asarray(inverse),
    )


def solution(mesh):
    return jax.shard_map(
        shards,
        mesh=mesh,
        in_specs=(P("region", "station", None, None), P(None, "region", None), P(None, "region")),
        out_specs=P(None, ("region", "station"), None),
        check_vma=False,
    )
```

```python
import math

import jax
import jax.numpy as jnp
import numpy as np
from jax import lax
from jax.experimental import pallas as pl
from jax.experimental.pallas import tpu as pltpu
from jax.sharding import PartitionSpec as P

MESH = pl.DeviceIdType.MESH
ROUNDS = 3
EVENTS = 16
GROUP = 4
COMP = 3
LENGTH = 512
LAGS = 256
SLOTS = 32
STATIONS = 16
EPS = 1e-06
CHUNK = COMP * EVENTS
TRACES = GROUP * CHUNK
PERIOD = LENGTH + LAGS // 2
HALF = PERIOD // 2
WIDE = 3 * LAGS
GRANT = 55200 * 2**10
HALVES = 2
SHIFT = 2
LEFT_OUT = SHIFT * EVENTS


def tables():
    order = np.arange(HALF)
    times = np.arange(LENGTH)[:, None]
    angle = 2.0 * np.pi * ((2 * order[None, :] + 1) * times % (2 * PERIOD)) / (2 * PERIOD)
    real, imag = np.cos(angle), -np.sin(angle)
    forward = np.concatenate([real[:, :256], imag[:, :256], real[:, 256:], imag[:, 256:]], axis=1)
    lags = np.arange(LAGS)[None, :] - LAGS // 2
    angle = 2.0 * np.pi * ((2 * order[:, None] + 1) * lags % (2 * PERIOD)) / (2 * PERIOD)
    factor = 2.0 / (PERIOD * math.sqrt(STATIONS * COMP * LENGTH))
    cos, sin = factor * np.cos(angle), factor * np.sin(angle)
    inverse = np.concatenate(
        [cos[:256], -sin[:256], cos[256:], cos[256:], -sin[256:], sin[256:]], axis=0
    )
    return forward.astype(jnp.bfloat16), inverse.astype(jnp.bfloat16)


def kernel(
    x_hbm, lists_hbm, counts_hbm, forward_hbm, inverse_hbm, out_ref,
    x_in, lists_ref, counts_ref, forward, inverse, normal, arrived, spectra, left, right, total,
    message, heard, picks, shares, gathered,
    load_sem, wave_out, wave_in, list_out, list_in, share_out, share_in, ready, settled,
):
    region, group = lax.axis_index("region"), lax.axis_index("station")
    z = lax.rem(region, 8)
    bits = [lax.rem(z // (1 << e), 2) for e in range(ROUNDS)]
    step = [(1 << e) * (1 - 2 * bits[e]) for e in range(ROUNDS)]
    partner = [region + step[0], region + step[1], region + step[1] + step[2]]
    mates = [lax.rem(group + d, GROUP) for d in range(GROUP)]
    late = bits[2]
    odd = lax.rem(bits[0] + bits[1] + bits[2], 2)
    worked, sent = odd * HALVES * CHUNK, (1 - odd) * HALVES * CHUNK

    arrived[1, HALVES * CHUNK :] = jnp.zeros_like(arrived[1, HALVES * CHUNK :])
    arrived[2, HALVES * CHUNK - LEFT_OUT :] = jnp.zeros_like(arrived[2, HALVES * CHUNK - LEFT_OUT :])
    barrier = pltpu.get_barrier_semaphore()

    def greet(which, to):
        pl.semaphore_signal(which, inc=1, device_id=to, device_id_type=MESH)

    greet(barrier, (partner[1], group))
    greet(barrier, (partner[0], group))
    for d in range(1, GROUP):
        greet(barrier, (region, mates[d]))

    @pl.when(late == 0)
    def _():
        greet(barrier, (partner[2], group))

    loads = [
        pltpu.make_async_copy(x_hbm, x_in, load_sem.at[0]),
        pltpu.make_async_copy(forward_hbm, forward, load_sem.at[1]),
        pltpu.make_async_copy(inverse_hbm, inverse, load_sem.at[2]),
        pltpu.make_async_copy(lists_hbm, lists_ref, load_sem.at[3]),
        pltpu.make_async_copy(counts_hbm, counts_ref, load_sem.at[4]),
    ]
    for k in (3, 0, 1, 2, 4):
        loads[k].start()

    loads[3].wait()
    message[...] = jnp.zeros_like(message)
    for e in range(ROUNDS):
        message[2 * e : 2 * e + 2, 0:SLOTS] = lists_ref[e]
    mine = message[...]
    turned = pltpu.roll(mine, SLOTS, 1)
    even = lax.rem(lax.broadcasted_iota(jnp.int32, (8, 128), 0), 2) == 0
    turned = jnp.where(even, pltpu.roll(turned, 7, 0), pltpu.roll(turned, 1, 0))
    message[...] = mine + turned

    row = lax.broadcasted_iota(jnp.int32, (TRACES, TRACES), 0)
    column = lax.broadcasted_iota(jnp.int32, (TRACES, TRACES), 1)
    source = lax.rem(row, EVENTS) * (COMP * GROUP) + lax.rem(row // EVENTS, COMP) * GROUP + row // CHUNK
    reorder = jnp.where(column == source, 1.0, 0.0).astype(jnp.bfloat16)
    loads[0].wait()
    traces = x_in[...].astype(jnp.float32).reshape(TRACES, LENGTH)
    traces = traces - jnp.mean(traces, axis=-1, keepdims=True)
    traces = traces * lax.rsqrt(jnp.mean(traces * traces, axis=-1, keepdims=True) + EPS)
    normal[...] = jnp.dot(
        reorder, traces.astype(jnp.bfloat16), preferred_element_type=jnp.float32
    ).astype(jnp.bfloat16)

    def rows(base, h):
        return pl.ds(pl.multiple_of(base + h * CHUNK, CHUNK), CHUNK)

    def copy(e, h, src, dst, size):
        return pltpu.make_async_remote_copy(
            src_ref=normal.at[pl.ds(pl.multiple_of(src, EVENTS), size)],
            dst_ref=arrived.at[e, pl.ds(dst, size)],
            send_sem=wave_out.at[e, h],
            recv_sem=wave_in.at[e, h],
            device_id=(partner[e], group),
            device_id_type=MESH,
        )

    last = HALVES * CHUNK - LEFT_OUT

    def wave(e, h):
        if e < 2:
            if h < HALVES:
                return copy(e, h, sent + h * CHUNK, h * CHUNK, CHUNK)
            return copy(e, h, worked + last, last + CHUNK, LEFT_OUT)
        if h == 0:
            return copy(e, h, worked, 0, CHUNK)
        if h == 1:
            return copy(e, h, worked + CHUNK, CHUNK, CHUNK - LEFT_OUT)
        if h == 2:
            return copy(e, h, worked + last, last, LEFT_OUT)
        return copy(e, h, sent + last, last + CHUNK, LEFT_OUT)

    def listing(e):
        return pltpu.make_async_remote_copy(
            src_ref=message,
            dst_ref=heard.at[e],
            send_sem=list_out.at[e],
            recv_sem=list_in.at[e],
            device_id=(partner[e], group),
            device_id_type=MESH,
        )

    def share(e, side, d):
        near = partner[1] if e == 2 else region
        to = near + side * (partner[e] - near)
        return pltpu.make_async_remote_copy(
            src_ref=shares.at[e, GROUP * side + mates[d]],
            dst_ref=gathered.at[e, GROUP * side + group],
            send_sem=share_out.at[e],
            recv_sem=share_in.at[e],
            device_id=(to, mates[d]),
            device_id_type=MESH,
        )

    def all_shares(e):
        size = 2 * GROUP if e == 2 else 2 * GROUP - 1
        return pltpu.make_async_remote_copy(
            src_ref=shares.at[e, pl.ds(0, size)],
            dst_ref=gathered.at[e, pl.ds(0, size)],
            send_sem=share_out.at[e],
            recv_sem=share_in.at[e],
            device_id=(partner[e], group),
            device_id_type=MESH,
        )

    def send(e):
        listing(e).start()
        for h in range(HALVES):
            wave(e, h).start()

    @pl.when(late == 0)
    def _():
        pl.semaphore_wait(barrier, 5)

    @pl.when(late == 1)
    def _():
        pl.semaphore_wait(barrier, 6)
        greet(ready, (partner[2], group))
        send(2)
        wave(2, 2).start()
        wave(2, 3).start()

    send(1)
    send(0)

    @pl.when(late == 0)
    def _():
        wave(1, 2).start()

    loads[1].wait()
    spectra[0, : HALVES * CHUNK] = jnp.dot(
        normal[pl.ds(pl.multiple_of(worked, CHUNK), HALVES * CHUNK)], forward[...], preferred_element_type=jnp.float32
    ).astype(jnp.bfloat16)
    loads[2].wait()
    loads[4].wait()

    @pl.when(late == 0)
    def _():
        pl.semaphore_wait(ready, 1)
        send(2)

    for d in range(1, GROUP):
        greet(settled, (region, mates[d]))

    lane = lax.broadcasted_iota(jnp.int32, (8, 128), 1)
    cell = lax.broadcasted_iota(jnp.int32, (COMP * 2 * SLOTS, CHUNK), 1)
    part = lax.broadcasted_iota(jnp.int32, (COMP * 2 * SLOTS, CHUNK), 0) // (2 * SLOTS) * EVENTS
    theirs_row = lax.broadcasted_iota(jnp.int32, (2 * SLOTS, LAGS), 0) >= SLOTS

    def work(e):
        listing(e).wait_recv()
        events = jnp.where(lane < SLOTS, heard[1] if e == 2 else message[...], heard[e]).astype(jnp.float32).T
        for side in range(2):
            event = events[: 2 * SLOTS, 2 * e + side : 2 * e + side + 1].astype(jnp.int32)
            event = jnp.concatenate([event] * COMP, axis=0)
            picks[side] = jnp.where(cell == part + event, 1.0, 0.0).astype(jnp.bfloat16)
        total[...] = jnp.zeros_like(total)
        known = 2 if e == 2 else 0

        def pick_left(h):
            left[h] = jnp.dot(picks[0], spectra[known, h * CHUNK : (h + 1) * CHUNK], preferred_element_type=jnp.float32)

        for h in range(HALVES):
            pick_left(h)
        if e == 2:

            @pl.when(late == 0)
            def _():
                wave(1, 2).wait_recv()
                spectra[2, HALVES * CHUNK :] = jnp.dot(
                    arrived[1, HALVES * CHUNK :], forward[...], preferred_element_type=jnp.float32
                ).astype(jnp.bfloat16)
                pick_left(2)

        def unit(h):
            spectra[1 + e, h * CHUNK : (h + 1) * CHUNK] = jnp.dot(
                arrived[e, h * CHUNK : (h + 1) * CHUNK], forward[...], preferred_element_type=jnp.float32
            ).astype(jnp.bfloat16)
            right[...] = jnp.dot(picks[1], spectra[1 + e, h * CHUNK : (h + 1) * CHUNK], preferred_element_type=jnp.float32)
            for g in range(2 * SLOTS // 16):
                to = pl.ds(16 * g, 16)
                sums = [total[to, 0:256], total[to, 256:512], total[to, 512:640], total[to, 640:768]]
                for c in range(COMP):
                    at = pl.ds(c * 2 * SLOTS + 16 * g, 16)
                    lr, li, lm = left[h, at, 0:256], left[h, at, 256:512], left[h, at, 512:640]
                    rr, ri, rm = right[at, 0:256], right[at, 256:512], right[at, 512:640]
                    sums[0] += lr * rr + li * ri
                    sums[1] += lr * ri - li * rr
                    sums[2] += lm * rm
                    sums[3] += lm * pltpu.roll(rm, 64, 1)
                total[to, 0:256], total[to, 256:512], total[to, 512:640], total[to, 640:768] = sums

        for h in range(HALVES):
            wave(e, h).wait_recv()
            if e == 2 and h == 1:

                @pl.when(late == 0)
                def _():
                    wave(2, 2).wait_recv()

            unit(h)
        if e == 2:

            @pl.when(late == 0)
            def _():
                wave(2, 3).wait_recv()
                unit(2)

        if e == 2:
            for turn in range(2):
                side = 1 - late if turn else late
                half = pl.ds(pl.multiple_of(side * SLOTS, SLOTS), SLOTS)
                sign = (1 - 2 * side) * jnp.ones((SLOTS, LAGS), jnp.float32)
                real, imag, both, cross = total[half, 0:256], total[half, 256:512], total[half, 512:640], total[half, 640:768]
                curves = jnp.dot(
                    jnp.concatenate([real, imag * sign, both, cross * sign[:, :128]], axis=1).astype(jnp.bfloat16),
                    inverse[...],
                    preferred_element_type=jnp.float32,
                )
                for k in range(GROUP):
                    piece = curves[8 * k : 8 * k + 8]
                    shares[e, GROUP * side + k] = jnp.concatenate([piece[:, :128], piece[:, 128:]], axis=0).astype(jnp.bfloat16)
                for d in range(GROUP):
                    if e == 2 or turn == 0 or d > 0:
                        share(e, side, d).start()

        else:
            real, imag, both, cross = total[:, 0:256], total[:, 256:512], total[:, 512:640], total[:, 640:768]
            imag = jnp.where(theirs_row, -imag, imag)
            cross = jnp.where(theirs_row[:, :128], -cross, cross)
            curves = jnp.dot(
                jnp.concatenate([real, imag, both, cross], axis=1).astype(jnp.bfloat16),
                inverse[...],
                preferred_element_type=jnp.float32,
            )
            for k in range(2 * GROUP):
                piece = curves[8 * k : 8 * k + 8]
                shares[e, k] = jnp.concatenate([piece[:, :128], piece[:, 128:]], axis=0).astype(jnp.bfloat16)
            for side in range(2):
                for d in range(GROUP):
                    if e == 2 or side == 1 or d > 0:
                        share(e, side, d).start()

        if e < 2:
            gathered[e, pl.ds(group, 1)] = shares[e, pl.ds(group, 1)]

    pl.semaphore_wait(settled, GROUP - 1)
    work(1)

    @pl.when(late == 0)
    def _():
        work(0)

    work(2)

    @pl.when(late == 1)
    def _():
        work(0)

    for e in range(ROUNDS):
        listing(e).wait_send()
        for h in range(HALVES):
            wave(e, h).wait_send()

    @pl.when(late == 0)
    def _():
        wave(1, 2).wait_send()

    @pl.when(late == 1)
    def _():
        wave(2, 2).wait_send()
        wave(2, 3).wait_send()


    slot = group * 8 + lax.rem(lax.broadcasted_iota(jnp.int32, (16, 128), 0), 8)
    for e in range(ROUNDS):
        all_shares(e).wait_recv()
        curve = jnp.sum(gathered[e].astype(jnp.float32), axis=0)
        curve = jnp.where(slot < counts_ref[0, e], curve, 0.0)
        out_ref[e, :, 0:128] = curve[0:8]
        out_ref[e, :, 128:256] = curve[8:16]

    for e in range(ROUNDS):
        all_shares(e).wait_send()


def shards(waveforms, pair_lists, pair_counts):
    forward, inverse = tables()
    bf16, f32 = jnp.bfloat16, jnp.float32
    dma = pltpu.SemaphoreType.DMA
    return pl.pallas_call(
        kernel,
        out_shape=jax.ShapeDtypeStruct((ROUNDS, 8, LAGS), f32),
        in_specs=[
            pl.BlockSpec(memory_space=pl.ANY),
            pl.BlockSpec(memory_space=pl.ANY),
            pl.BlockSpec(memory_space=pl.ANY),
            pl.BlockSpec(memory_space=pl.ANY),
            pl.BlockSpec(memory_space=pl.ANY),
        ],
        out_specs=pl.BlockSpec(memory_space=pltpu.VMEM),
        scratch_shapes=[
            pltpu.VMEM((EVENTS, COMP, GROUP, LENGTH), bf16),
            pltpu.VMEM((ROUNDS, 2, SLOTS), jnp.int32),
            pltpu.SMEM((1, ROUNDS), jnp.int32),
            pltpu.VMEM((LENGTH, PERIOD), bf16),
            pltpu.VMEM((WIDE, LAGS), bf16),
            pltpu.VMEM((TRACES, LENGTH), bf16),
            pltpu.VMEM((ROUNDS, (HALVES + 1) * CHUNK, LENGTH), bf16),
            pltpu.VMEM((1 + ROUNDS, (HALVES + 1) * CHUNK, PERIOD), bf16),
            pltpu.VMEM((HALVES + 1, COMP * 2 * SLOTS, PERIOD), f32),
            pltpu.VMEM((COMP * 2 * SLOTS, PERIOD), f32),
            pltpu.VMEM((2 * SLOTS, WIDE), f32),
            pltpu.VMEM((8, 128), jnp.int32),
            pltpu.VMEM((ROUNDS, 8, 128), jnp.int32),
            pltpu.VMEM((2, COMP * 2 * SLOTS, CHUNK), bf16),
            pltpu.VMEM((ROUNDS, 2 * GROUP, 16, 128), bf16),
            pltpu.VMEM((ROUNDS, 2 * GROUP, 16, 128), bf16),
            dma((5,)),
            dma((ROUNDS, 2 * HALVES)),
            dma((ROUNDS, 2 * HALVES)),
            dma((ROUNDS,)),
            dma((ROUNDS,)),
            dma((ROUNDS,)),
            dma((ROUNDS,)),
            pltpu.SemaphoreType.REGULAR,
            pltpu.SemaphoreType.REGULAR,
        ],
        compiler_params=pltpu.CompilerParams(
            collective_id=0, has_side_effects=True, vmem_limit_bytes=GRANT
        ),
        name="correlate",
    )(
        jnp.transpose(waveforms, (0, 2, 1, 3)),
        pltpu.with_memory_space_constraint(jnp.transpose(pair_lists, (0, 2, 1)), pltpu.HBM),
        pltpu.with_memory_space_constraint(jnp.transpose(pair_counts, (1, 0)), pltpu.HBM),
        jnp.asarray(forward),
        jnp.asarray(inverse),
    )


def solution(mesh):
    return jax.shard_map(
        shards,
        mesh=mesh,
        in_specs=(P("region", "station", None, None), P(None, "region", None), P(None, "region")),
        out_specs=P(None, ("region", "station"), None),
        check_vma=False,
    )
```
